512 devices in a mesh: wide: 64 (over x, y_hi, z), narrow: 8 (over y_lo, core).
Axes of the slice: x: 4, y: 8 (y_hi: 2, y_lo: 4; y = y_hi * 4 + y_lo), z: 8, core: 2. Of those that a mesh axis runs over, the one named last changes fastest.
Arguments:
- query_rows: bfloat16 [65536, 512], P(('wide', 'narrow')), may hold values from -6 to 6
- key_rows: bfloat16 [65536, 512], P(('wide', 'narrow')), may hold values from -6 to 6
- value_rows: bfloat16 [65536, 512], P(('wide', 'narrow')), may hold values from -6 to 6
- out_grad: bfloat16 [65536, 512], P(('wide', 'narrow')), may hold values from -6 to 6
- doc_lengths: int32 [1024], replicated, may hold values from 1 to 40960, 65536 in all
- projection: float32 [128, 64], replicated, may hold values from -6 to 6
Outputs:
- attended: bfloat16 [65536, 512], P(('wide', 'narrow'))
- query_grad: bfloat16 [65536, 512], P(('wide', 'narrow'))
- key_grad: bfloat16 [65536, 512], P(('wide', 'narrow'))
- value_grad: bfloat16 [65536, 512], P(('wide', 'narrow'))
The draws below stay inside these ranges and needn't reach their ends.
Inputs may be any that keep to these rules, and one draw needn't show every extreme that they name: `doc_lengths`: positive document lengths that sum to 65536; the longest is exactly 40960.
All inputs are finite; a program needn't handle non-finite values.
Results may differ from the reference program's by a relative error of at most 0.0053.
Values may be sent and summed in bfloat16 or wider, within the bound.
A program may use at most 128 MiB of HBM per device.

```python
import math
import jax
import jax.numpy as jnp
import numpy as np
from jax import lax

HEADS = 8
HEAD_DIM = 64
FEATURES = 128
TOKENS = 65536
DOCS = 1024
MOST_LEN = 40960


def levels(stream_key, dims, cuts, least, high):
    factor_of, own = 1.0, jax.random.fold_in(stream_key, 6)
    for axis_at, blocks in cuts:
        draws = jnp.exp(jax.random.uniform(jax.random.fold_in(own, axis_at), (blocks,), jnp.float32, least / len(cuts), high / len(cuts)))
        factor_of = factor_of * jnp.repeat(draws, dims[axis_at] // blocks).reshape([-1 if axis == axis_at else 1 for axis in range(len(dims))])
    return factor_of


def profile(number_of, total, most, lean):
    loads = [(1 << 20) // math.isqrt(grade ** lean) + 1 for grade in range(2, number_of + 1)]
    spare, counts = total - most - (number_of - 1), [1] * (number_of - 1)
    while spare > 0:
        free = [i for i in range(number_of - 1) if counts[i] < most]
        whole, budget = sum([loads[i] for i in free]), spare
        for i in free:
            addition = min(most - counts[i], max(1, budget * loads[i] // whole), spare)
            counts[i] = counts[i] + addition
            spare = spare - addition
    return np.array([most] + counts)


def ragged_sizes(key, amount, total, reach, skew):
    if amount == 2:
        one = jax.random.randint(key, (), max(1, total - reach), min(reach, total - 1) + 1)
        return jnp.stack([one, total - one])
    sizes = jnp.asarray(profile(amount, total, reach, skew), jnp.int32)
    couples = (amount - 1) // 2
    source_of, receiver = sizes[1:1 + 2 * couples:2], sizes[2:2 + 2 * couples:2]
    slack = jnp.minimum(source_of - 1, reach - receiver)
    moved = jax.random.randint(jax.random.fold_in(key, 1), (couples,), 0, 1 << 20) % (slack + 1)
    sizes = sizes.at[1:1 + 2 * couples:2].set(source_of - moved).at[2:2 + 2 * couples:2].set(receiver + moved)
    return sizes[jax.random.permutation(jax.random.fold_in(key, 2), amount)]


def normal_values(stream_key, extent, scale, reach, pieces=(), kind=jnp.bfloat16):
    factor_of = levels(stream_key, extent, pieces, -0.22, 0.18) if pieces else 1.0
    values = jax.random.normal(stream_key, extent, jnp.float32) * scale * factor_of
    return jnp.minimum(jnp.maximum(values, -reach), reach).astype(kind)


def setup_inputs(seed: int = 0) -> dict:
    splits = jax.random.split(jax.random.key(seed), 7)
    return {
        "query_rows": normal_values(splits[0], (TOKENS, HEADS * HEAD_DIM), 1.0, 6.0, ((0, 512),)),
        "key_rows": normal_values(splits[1], (TOKENS, HEADS * HEAD_DIM), 1.0, 6.0, ((0, 512),)),
        "value_rows": normal_values(splits[2], (TOKENS, HEADS * HEAD_DIM), 1.0, 6.0, ((0, 512),)),
        "out_grad": normal_values(splits[3], (TOKENS, HEADS * HEAD_DIM), 1.0, 6.0, ((0, 512),)),
        "doc_lengths": ragged_sizes(splits[4], DOCS, TOKENS, MOST_LEN, 2).astype(jnp.int32),
        "projection": normal_values(splits[5], (FEATURES, HEAD_DIM), 1.0, 6.0, (), jnp.float32),
    }


HIGHEST_PRECISION = lax.Precision.HIGHEST
feature_floor = 1e-06

def split_heads(matrix):
    count = matrix.shape[0]
    return jnp.transpose(matrix.reshape(count, HEADS, HEAD_DIM), (1, 0, 2))

def merge_heads(tensor):
    return jnp.transpose(tensor, (1, 0, 2)).reshape(tensor.shape[1], HEADS * HEAD_DIM).astype(jnp.bfloat16)

def positive_features(scaled, projection):
    mixed = jnp.einsum('hre,me->hrm', scaled, projection, precision=HIGHEST_PRECISION)
    half_norm = 0.5 * lax.optimization_barrier(jnp.sum(scaled * scaled, axis=-1, keepdims=True))
    factor = 1.0 / math.sqrt(FEATURES)
    exponent = jnp.exp(mixed - half_norm) * factor
    return (exponent, (exponent + feature_floor * factor).astype(jnp.bfloat16))

def feature_grad(scaled, exponent, upstream, projection):
    weighted = exponent * upstream
    back_proj = jnp.einsum('hrm,me->hre', weighted, projection, precision=HIGHEST_PRECISION)
    return (back_proj - scaled * lax.optimization_barrier(jnp.sum(weighted, axis=-1, keepdims=True))) * HEAD_DIM ** (-0.25)

def masked_state(weights, features, vectors):
    return jnp.einsum('hrm,hre->hme', features * weights[None, :, None], vectors, precision=HIGHEST_PRECISION)

def masked_total(weights, features):
    return jnp.einsum('r,hrm->hm', weights, features, precision=HIGHEST_PRECISION)

def masked_bias_total(weights, features, biases):
    return jnp.einsum('hr,hrm->hm', biases * weights[None, :], features, precision=HIGHEST_PRECISION)

def chain_step(carry, element):
    state, total = carry
    piece_state, piece_total, flag = element
    keep = flag[0] > 0
    renewed = (jnp.where(keep, piece_state, state + piece_state), jnp.where(keep, piece_total, total + piece_total))
    return (renewed, carry)

def reference(query_rows, key_rows, value_rows, out_grad, doc_lengths, projection):
    block_rows = 256
    block_count = TOKENS // block_rows
    starts = (jnp.cumsum(doc_lengths) - doc_lengths).astype(jnp.int32)
    opens_all = jnp.zeros((TOKENS,), jnp.int32).at[starts].set(1)
    doc_all = (jnp.cumsum(opens_all) - 1).astype(jnp.int32)
    inv_root = HEAD_DIM ** (-0.25)
    block_ids = jnp.arange(block_count, dtype=jnp.int32)

    def context(block_index):
        first_row = (block_index * block_rows).astype(jnp.int32)

        def rows_of(array):
            return lax.dynamic_slice_in_dim(array, first_row, block_rows, 0)
        doc_ids = rows_of(doc_all)
        opens = rows_of(opens_all).astype(jnp.float32)
        query_scaled = split_heads(rows_of(query_rows)).astype(jnp.float32) * inv_root
        key_scaled = split_heads(rows_of(key_rows)).astype(jnp.float32) * inv_root
        query_exp, query_phi = positive_features(query_scaled, projection)
        key_exp, key_phi = positive_features(key_scaled, projection)
        return {'same_doc': (doc_ids[:, None] == doc_ids[None, :]).astype(jnp.float32), 'front_use': (doc_ids == doc_ids[0]).astype(jnp.float32) * (1.0 - opens[0]), 'back_use': (doc_ids == doc_ids[block_rows - 1]).astype(jnp.float32), 'reset': jnp.max(opens).reshape(1), 'query_scaled': query_scaled, 'key_scaled': key_scaled, 'value_heads': split_heads(rows_of(value_rows)).astype(jnp.float32), 'grad_heads': split_heads(rows_of(out_grad)).astype(jnp.float32), 'query_exp': query_exp, 'key_exp': key_exp, 'query_phi': query_phi.astype(jnp.float32), 'key_phi': key_phi.astype(jnp.float32)}

    def section_pieces(block_index):
        data = context(block_index)
        back_piece = (masked_state(data['back_use'], data['key_phi'], data['value_heads']), masked_total(data['back_use'], data['key_phi']), data['reset'])
        front_piece = (masked_state(data['front_use'], data['key_phi'], data['value_heads']), masked_total(data['front_use'], data['key_phi']), data['reset'])
        return (back_piece, front_piece)
    zero_state = (jnp.zeros((HEADS, FEATURES, HEAD_DIM), jnp.float32), jnp.zeros((HEADS, FEATURES), jnp.float32))
    back_pieces, front_pieces = lax.map(section_pieces, block_ids)
    unused_end, before = lax.scan(chain_step, zero_state, back_pieces)
    unused_start, after = lax.scan(chain_step, zero_state, front_pieces, reverse=True)

    def scores_of(data):
        return jnp.einsum('hrm,hsm->hrs', data['query_phi'], data['key_phi'], precision=HIGHEST_PRECISION) * data['same_doc'][None]

    def section_forward(inputs):
        block_index, before_part, after_part = inputs
        data = context(block_index)
        scores = scores_of(data)
        front = data['front_use'][None, :, None]
        back = data['back_use'][None, :, None]
        query_phi = data['query_phi']
        numer = jnp.einsum('hrs,hse->hre', scores, data['value_heads'], precision=HIGHEST_PRECISION)
        numer = numer + front * jnp.einsum('hrm,hme->hre', query_phi, before_part[0], precision=HIGHEST_PRECISION)
        numer = numer + back * jnp.einsum('hrm,hme->hre', query_phi, after_part[0], precision=HIGHEST_PRECISION)
        denom = lax.optimization_barrier(jnp.sum(scores, axis=-1))
        denom = denom + front[..., 0] * jnp.einsum('hrm,hm->hr', query_phi, before_part[1], precision=HIGHEST_PRECISION)
        denom = denom + back[..., 0] * jnp.einsum('hrm,hm->hr', query_phi, after_part[1], precision=HIGHEST_PRECISION)
        attended_f = numer / denom[..., None]
        scaled_grad = data['grad_heads'] / denom[..., None]
        bias_term = -lax.optimization_barrier(jnp.sum(data['grad_heads'] * attended_f, axis=-1)) / denom
        grad_back = (masked_state(data['back_use'], query_phi, scaled_grad), masked_bias_total(data['back_use'], query_phi, bias_term), data['reset'])
        grad_front = (masked_state(data['front_use'], query_phi, scaled_grad), masked_bias_total(data['front_use'], query_phi, bias_term), data['reset'])
        return (merge_heads(attended_f), scaled_grad, bias_term, grad_back, grad_front)
    attended, scaled_grads, bias_terms, grad_backs, grad_fronts = lax.map(section_forward, (block_ids, before, after))
    unused_end2, grad_before = lax.scan(chain_step, zero_state, grad_backs)
    unused_start2, grad_after = lax.scan(chain_step, zero_state, grad_fronts, reverse=True)

    def section_backward(inputs):
        block_index, before_part, after_part, gb_part, ga_part, scaled_grad, bias_term = inputs
        data = context(block_index)
        scores = scores_of(data)
        front = data['front_use'][None, :, None]
        back = data['back_use'][None, :, None]
        query_phi = data['query_phi']
        key_phi = data['key_phi']
        value_heads = data['value_heads']
        coupling = (jnp.einsum('hre,hse->hrs', scaled_grad, value_heads, precision=HIGHEST_PRECISION) + bias_term[..., None]) * data['same_doc'][None]
        query_up = jnp.einsum('hrs,hsm->hrm', coupling, key_phi, precision=HIGHEST_PRECISION)
        query_up = query_up + front * (jnp.einsum('hme,hre->hrm', before_part[0], scaled_grad, precision=HIGHEST_PRECISION) + bias_term[..., None] * before_part[1][:, None, :])
        query_up = query_up + back * (jnp.einsum('hme,hre->hrm', after_part[0], scaled_grad, precision=HIGHEST_PRECISION) + bias_term[..., None] * after_part[1][:, None, :])
        key_up = jnp.einsum('hrs,hrm->hsm', coupling, query_phi, precision=HIGHEST_PRECISION)
        key_up = key_up + front * (jnp.einsum('hme,hse->hsm', gb_part[0], value_heads, precision=HIGHEST_PRECISION) + gb_part[1][:, None, :])
        key_up = key_up + back * (jnp.einsum('hme,hse->hsm', ga_part[0], value_heads, precision=HIGHEST_PRECISION) + ga_part[1][:, None, :])
        value_up = jnp.einsum('hrs,hre->hse', scores, scaled_grad, precision=HIGHEST_PRECISION)
        value_up = value_up + front * jnp.einsum('hme,hsm->hse', gb_part[0], key_phi, precision=HIGHEST_PRECISION)
        value_up = value_up + back * jnp.einsum('hme,hsm->hse', ga_part[0], key_phi, precision=HIGHEST_PRECISION)
        query_out = merge_heads(feature_grad(data['query_scaled'], data['query_exp'], query_up, projection))
        key_out = merge_heads(feature_grad(data['key_scaled'], data['key_exp'], key_up, projection))
        return (query_out, key_out, merge_heads(value_up))
    query_grad, key_grad, value_grad = lax.map(section_backward, (block_ids, before, after, grad_before, grad_after, scaled_grads, bias_terms))
    width = HEADS * HEAD_DIM
    return (attended.reshape(TOKENS, width), query_grad.reshape(TOKENS, width), key_grad.reshape(TOKENS, width), value_grad.reshape(TOKENS, width))
```

```python
import functools

import jax
import jax.numpy as jnp
from jax import lax
from jax.experimental import pallas as pl
from jax.experimental.pallas import tpu as pltpu
from jax.sharding import PartitionSpec as P

HEAD_DIM = 64
FEATURES = 128
LANES = 128
FLOOR = 1e-06
F32 = jnp.float32
BF16 = jnp.bfloat16
INV_ROOT = HEAD_DIM ** (-0.25)
FACTOR = FEATURES ** (-0.5)
VMEM_BYTES = 48 * 1024 * 1024
STRIP = 256


def dot(a, b, da, db):
    return lax.dot_general(a, b, (((da,), (db,)), ((), ())), preferred_element_type=F32)


def split2(x):
    high = x.astype(BF16)
    return high, (x - high.astype(F32)).astype(BF16)


def split3(x):
    high = x.astype(BF16)
    rest = x - high.astype(F32)
    mid = rest.astype(BF16)
    return high, mid, (rest - mid.astype(F32)).astype(BF16)


def dot_exact(a, b, da, db):
    high, low = split2(b)
    return dot(a, high, da, db) + dot(a, low, da, db)


def dot_wide(a, b, da, db):
    a0, a1 = split2(a)
    b0, b1 = split2(b)
    return dot(a0, b0, da, db) + dot(a0, b1, da, db) + dot(a1, b0, da, db)


def features(x, projection):
    parts = split3(projection * INV_ROOT)
    mixed = dot(x, parts[0], 1, 1) + dot(x, parts[1], 1, 1) + dot(x, parts[2], 1, 1)
    wide = x.astype(F32)
    half = jnp.sum(wide * wide, axis=1, keepdims=True) * (0.5 * INV_ROOT * INV_ROOT)
    expo = jnp.exp(mixed - half) * FACTOR
    return expo, (expo + FLOOR * FACTOR).astype(BF16)


def extended(x, extra):
    rows = x.shape[0]
    lane = lax.broadcasted_iota(jnp.int32, (rows, HEAD_DIM), 1)
    tail = jnp.where(lane == 0, jnp.broadcast_to(extra, (rows, HEAD_DIM)), 0.0)
    return jnp.concatenate([x, tail], axis=1)


def feature_grad(x, expo, up, projection):
    weighted = expo * up
    ones = extended(projection, jnp.ones((FEATURES, 1), F32))
    back = dot_wide(weighted, ones, 1, 0)
    scaled = x.astype(F32) * INV_ROOT
    return (back[:, :HEAD_DIM] - scaled * back[:, HEAD_DIM : HEAD_DIM + 1]) * INV_ROOT


def count_ends(ends, positions):
    return jnp.sum(jnp.where(ends <= positions, 1.0, 0.0), axis=1, keepdims=True)


def pack_kernel(q_ref, k_ref, v_ref, g_ref, kv_ref, qg_ref):
    for head in range(kv_ref.shape[0]):
        cols = slice(head * HEAD_DIM, (head + 1) * HEAD_DIM)
        kv_ref[head] = jnp.concatenate([k_ref[:, cols], v_ref[:, cols]], axis=1)
        qg_ref[head] = jnp.concatenate([q_ref[:, cols], g_ref[:, cols]], axis=1)


def unpack_kernel(first_ref, second_ref, out_a, out_b, out_c, out_d):
    for pair in range(first_ref.shape[0] // 2):
        cols = slice(pair * LANES, (pair + 1) * LANES)
        for ref, left, right in ((first_ref, out_a, out_b), (second_ref, out_c, out_d)):
            even, odd = ref[2 * pair], ref[2 * pair + 1]
            left[:, cols] = jnp.concatenate([even[:, :HEAD_DIM], odd[:, :HEAD_DIM]], axis=1)
            right[:, cols] = jnp.concatenate([even[:, HEAD_DIM:], odd[:, HEAD_DIM:]], axis=1)


def store_pieces(ref, back, front):
    owners = ref.shape[0]
    share = FEATURES // owners
    for i in range(share):
        ref[:, i, :] = back[i * owners : (i + 1) * owners]
        ref[:, share + i, :] = front[i * owners : (i + 1) * owners]


def load_pieces(ref):
    owners = ref.shape[0]
    share = FEATURES // owners
    before = jnp.concatenate([ref[:, i, :] for i in range(share)], axis=0)
    after = jnp.concatenate([ref[:, share + i, :] for i in range(share)], axis=0)
    return before, after


def key_kernel(place_ref, ends_ref, kv_ref, proj_ref, piece_ref, phi_ref, expo_ref, ids_ref, row_ref):
    rows = kv_ref.shape[0]
    first = place_ref[0] * rows
    ends = ends_ref[...]
    for strip in range(rows // STRIP):
        at = slice(strip * STRIP, (strip + 1) * STRIP)
        place = lax.broadcasted_iota(jnp.int32, (STRIP, 1), 0) + (first + strip * STRIP)
        ids_ref[at, :] = jnp.broadcast_to(count_ends(ends, place), (STRIP, LANES))
        expo, phi = features(kv_ref[at, :HEAD_DIM], proj_ref[...])
        expo_ref[at, :] = expo
        phi_ref[at, :] = phi
    ids = ids_ref[...]
    row_ref[...] = jnp.transpose(ids)[:8, :]
    front = ids == ids[:1, :]
    back = ids == ids[rows - 1 :, :]
    vectors = extended(kv_ref[:, HEAD_DIM:].astype(F32), jnp.ones((rows, 1), F32))
    both = jnp.concatenate([jnp.where(back, vectors, 0.0), jnp.where(front, vectors, 0.0)], axis=1)
    pieces = dot(phi_ref[...], both.astype(BF16), 0, 0)
    store_pieces(piece_ref, pieces[:, :LANES], pieces[:, LANES:])


def chain_kernel(rows, ends_ref, in_ref, out_ref):
    owners = in_ref.shape[0]
    share = FEATURES // owners
    ends = ends_ref[...]
    block = lax.broadcasted_iota(jnp.int32, (LANES, 1), 0) * rows
    first = jnp.broadcast_to(count_ends(ends, block), (LANES, LANES))
    last = jnp.broadcast_to(count_ends(ends, block + (rows - 1)), (LANES, LANES))
    mine = lax.broadcasted_iota(jnp.int32, (LANES, LANES), 0)
    other = lax.broadcasted_iota(jnp.int32, (LANES, LANES), 1)
    rising = jnp.where((jnp.transpose(last) == first) & (other < mine), 1.0, 0.0)
    falling = jnp.where((jnp.transpose(first) == last) & (other > mine), 1.0, 0.0)
    rising = rising[:owners, :owners].astype(BF16)
    falling = falling[:owners, :owners].astype(BF16)
    for i in range(2 * share):
        chain = rising if i < share else falling
        parts = split3(in_ref[:, i, :])
        out_ref[:, i, :] = dot(chain, parts[0], 1, 0) + dot(chain, parts[1], 1, 0) + dot(chain, parts[2], 1, 0)


def query_kernel(
    kv_ref, qg_ref, proj_ref, phi_k_ref, ids_ref, row_ref, state_ref,
    done_ref, piece_ref, key_up_ref, value_up_ref,
    a_ref, phi_ref,
):
    rows = kv_ref.shape[0]
    before, after = load_pieces(state_ref)
    both = jnp.concatenate([before, after], axis=1)
    both_high, both_low = split2(both)
    phi_k = phi_k_ref[...]
    values = extended(kv_ref[:, HEAD_DIM:].astype(F32), jnp.ones((rows, 1), F32)).astype(BF16)
    id_row = row_ref[:1, :]
    id_first = ids_ref[:1, :]
    id_last = ids_ref[rows - 1 :, :]
    for strip in range(rows // STRIP):
        at = slice(strip * STRIP, (strip + 1) * STRIP)
        ids = ids_ref[at, :]
        front = ids == id_first
        back = ids == id_last
        mask = ids[:, :1] == id_row
        query = qg_ref[at, :HEAD_DIM]
        grad = qg_ref[at, HEAD_DIM:].astype(F32)
        expo, phi = features(query, proj_ref[...])
        phi_ref[at, :] = phi
        scores = jnp.where(mask, dot(phi, phi_k, 1, 1), 0.0)
        score_high, score_low = split2(scores)
        total = dot(score_high, values, 1, 0) + dot(score_low, values, 1, 0)
        far = dot(phi, both_high, 1, 0) + dot(phi, both_low, 1, 0)
        total = total + jnp.where(front, far[:, :LANES], 0.0) + jnp.where(back, far[:, LANES:], 0.0)
        inverse = 1.0 / total[:, HEAD_DIM : HEAD_DIM + 1]
        attended = total[:, :HEAD_DIM] * inverse
        bias = -jnp.sum(grad * attended, axis=1, keepdims=True) * inverse
        a = extended(grad * inverse, bias)
        a_ref[at, :] = a
        a_high, a_low = split2(a)
        coupling = jnp.where(mask, dot(a_high, values, 1, 1) + dot(a_low, values, 1, 1), 0.0)
        coupling_high, coupling_low = split2(coupling)
        up = dot(coupling_high, phi_k, 1, 0) + dot(coupling_low, phi_k, 1, 0)
        up = up + jnp.where(front, dot_wide(a, before, 1, 1), 0.0)
        up = up + jnp.where(back, dot_wide(a, after, 1, 1), 0.0)
        query_grad = feature_grad(query, expo, up, proj_ref[...])
        done_ref[at, :] = jnp.concatenate([attended, query_grad], axis=1).astype(BF16)
        key_up = dot(phi, coupling_high, 0, 0) + dot(phi, coupling_low, 0, 0)
        value_up = dot(a_high, score_high, 0, 0) + dot(a_low, score_high, 0, 0) + dot(a_high, score_low, 0, 0)
        if strip == 0:
            key_up_ref[...] = key_up
            value_up_ref[...] = value_up
        else:
            key_up_ref[...] += key_up
            value_up_ref[...] += value_up
    ids = ids_ref[...]
    a = a_ref[...]
    sides = jnp.concatenate(
        [jnp.where(ids == id_last, a, 0.0), jnp.where(ids == id_first, a, 0.0)], axis=1
    )
    high, low = split2(sides)
    phi = phi_ref[...]
    pieces = dot(phi, high, 0, 0) + dot(phi, low, 0, 0)
    store_pieces(piece_ref, pieces[:, :LANES], pieces[:, LANES:])


def finish_kernel(
    kv_ref, proj_ref, phi_k_ref, expo_ref, ids_ref, state_ref, key_up_ref, value_up_ref, done_ref
):
    rows = kv_ref.shape[0]
    before, after = load_pieces(state_ref)
    both_high, both_low = split2(jnp.concatenate([before, after], axis=1))
    rows_high, rows_low = split2(jnp.concatenate([before, after], axis=0))
    id_first = ids_ref[:1, :]
    id_last = ids_ref[rows - 1 :, :]
    for strip in range(rows // STRIP):
        at = slice(strip * STRIP, (strip + 1) * STRIP)
        ids = ids_ref[at, :]
        front = ids == id_first
        back = ids == id_last
        phi = phi_k_ref[at, :]
        values = extended(kv_ref[at, HEAD_DIM:].astype(F32), jnp.ones((STRIP, 1), F32)).astype(BF16)
        far_key = dot(values, rows_high, 1, 1) + dot(values, rows_low, 1, 1)
        up = jnp.transpose(key_up_ref[:, at])
        up = up + jnp.where(front, far_key[:, :LANES], 0.0) + jnp.where(back, far_key[:, LANES:], 0.0)
        far = dot(phi, both_high, 1, 0) + dot(phi, both_low, 1, 0)
        total = jnp.transpose(value_up_ref[:, at])
        total = total + jnp.where(front, far[:, :LANES], 0.0) + jnp.where(back, far[:, LANES:], 0.0)
        key_grad = feature_grad(kv_ref[at, :HEAD_DIM], expo_ref[at, :], up, proj_ref[...])
        done_ref[at, :] = jnp.concatenate([key_grad, total[:, :HEAD_DIM]], axis=1).astype(BF16)


def call(kernel, outs, operands, flops, scratch=()):
    in_specs = [
        pl.BlockSpec(memory_space=pltpu.SMEM if x.ndim == 1 else pltpu.VMEM) for x in operands
    ]
    moved = sum(x.size * x.dtype.itemsize for x in operands)
    moved += sum(x.size * x.dtype.itemsize for x in outs)
    return pl.pallas_call(
        kernel,
        out_shape=tuple(outs),
        in_specs=in_specs,
        out_specs=tuple(pl.BlockSpec(memory_space=pltpu.VMEM) for _ in outs),
        scratch_shapes=list(scratch),
        compiler_params=pltpu.CompilerParams(vmem_limit_bytes=VMEM_BYTES),
        cost_estimate=pl.CostEstimate(flops=flops, bytes_accessed=moved, transcendentals=0),
    )(*operands)


def exchange(x, axis):
    return lax.all_to_all(x, axis, split_axis=0, concat_axis=0, tiled=True)


def body(coarse, fine, query_rows, key_rows, value_rows, out_grad, doc_lengths, projection):
    own = query_rows.shape[0]
    heads = query_rows.shape[1] // HEAD_DIM
    rows = own * fine
    shape = jax.ShapeDtypeStruct
    packed = shape((heads, own, LANES), BF16)
    place = lax.axis_index("wide").reshape(1).astype(jnp.int32)
    ends = jnp.cumsum(doc_lengths).reshape(1, -1)

    kv, qg = call(pack_kernel, (packed, packed), (query_rows, key_rows, value_rows, out_grad), 0)
    kv = exchange(kv, "narrow").reshape(rows, LANES)
    qg = exchange(qg, "narrow").reshape(rows, LANES)

    pieces = shape((coarse, 2 * FEATURES // coarse, LANES), F32)
    full = shape((rows, LANES), F32)
    turned = shape((LANES, rows), F32)
    piece, phi_k, expo_k, ids, id_row = call(
        key_kernel,
        (pieces, shape((rows, LANES), BF16), full, full, shape((8, rows), F32)),
        (place, ends, kv, projection),
        2 * rows * LANES * LANES * 3,
    )
    chain = functools.partial(chain_kernel, rows)
    (moved,) = call(chain, (pieces,), (ends, exchange(piece, "wide")), 2 * coarse * coarse * 6 * LANES)
    state = exchange(moved, "wide")

    finished = shape((rows, LANES), BF16)
    done_q, piece_g, key_up, value_up = call(
        query_kernel,
        (finished, pieces, turned, turned),
        (kv, qg, projection, phi_k, ids, id_row, state),
        2 * rows * rows * LANES * 12,
        (pltpu.VMEM((rows, LANES), F32), pltpu.VMEM((rows, LANES), BF16)),
    )
    back_q = exchange(done_q.reshape(fine, own, LANES), "narrow")
    (moved_g,) = call(chain, (pieces,), (ends, exchange(piece_g, "wide")), 2 * coarse * coarse * 6 * LANES)
    state_g = exchange(moved_g, "wide")
    (done_k,) = call(
        finish_kernel,
        (finished,),
        (kv, projection, phi_k, expo_k, ids, state_g, key_up, value_up),
        2 * rows * LANES * LANES * 8,
    )
    back_k = exchange(done_k.reshape(fine, own, LANES), "narrow")
    out = shape(query_rows.shape, BF16)
    return call(unpack_kernel, (out, out, out, out), (back_q, back_k), 0)


def solution(mesh):
    tokens = P(("wide", "narrow"), None)
    return jax.shard_map(
        functools.partial(body, mesh.shape["wide"], mesh.shape["narrow"]),
        mesh=mesh,
        in_specs=(tokens, tokens, tokens, tokens, P(), P()),
        out_specs=(tokens, tokens, tokens, tokens),
        check_vma=False,
    )
```

```python
import functools

import jax
import jax.numpy as jnp
from jax import lax
from jax.experimental import pallas as pl
from jax.experimental.pallas import tpu as pltpu
from jax.sharding import PartitionSpec as P

HEAD_DIM = 64
FEATURES = 128
LANES = 128
FLOOR = 1e-06
F32 = jnp.float32
BF16 = jnp.bfloat16
INV_ROOT = HEAD_DIM ** (-0.25)
FACTOR = FEATURES ** (-0.5)
VMEM_BYTES = 56 * 1024 * 1024
MESH = pl.DeviceIdType.MESH
STRIP = 256


def dot(a, b, da, db):
    return lax.dot_general(a, b, (((da,), (db,)), ((), ())), preferred_element_type=F32)


def split2(x):
    high = x.astype(BF16)
    return high, (x - high.astype(F32)).astype(BF16)


def split3(x):
    high = x.astype(BF16)
    rest = x - high.astype(F32)
    mid = rest.astype(BF16)
    return high, mid, (rest - mid.astype(F32)).astype(BF16)


def beside(*parts):
    return jnp.concatenate(parts, axis=1)


def features(x, parts):
    mixed = dot(beside(x, x, x, jnp.zeros_like(x)), parts, 1, 0)
    wide = x.astype(F32)
    half = jnp.sum(wide * wide, axis=1, keepdims=True) * (0.5 * INV_ROOT * INV_ROOT)
    expo = jnp.exp(mixed - half) * FACTOR
    return expo, (expo + FLOOR * FACTOR).astype(BF16)


def extended(x, extra):
    rows = x.shape[0]
    lane = lax.broadcasted_iota(jnp.int32, (rows, HEAD_DIM), 1)
    tail = jnp.where(lane == 0, jnp.broadcast_to(extra, (rows, HEAD_DIM)), 0.0)
    return jnp.concatenate([x, tail], axis=1)


def feature_grad(x, expo, up, parts):
    high, low = split2(expo * up)
    back = dot(beside(high, low), beside(parts[0], parts[0]), 1, 1) + dot(high, parts[1], 1, 1)
    scaled = x.astype(F32) * INV_ROOT
    return (back[:, :HEAD_DIM] - scaled * back[:, HEAD_DIM : HEAD_DIM + 1]) * INV_ROOT


def unpack_kernel(first_ref, second_ref, out_a, out_b, out_c, out_d):
    for pair in range(first_ref.shape[0] // 2):
        cols = slice(pair * LANES, (pair + 1) * LANES)
        for ref, left, right in ((first_ref, out_a, out_b), (second_ref, out_c, out_d)):
            even, odd = ref[2 * pair], ref[2 * pair + 1]
            left[:, cols] = jnp.concatenate([even[:, :HEAD_DIM], odd[:, :HEAD_DIM]], axis=1)
            right[:, cols] = jnp.concatenate([even[:, HEAD_DIM:], odd[:, HEAD_DIM:]], axis=1)


def ends_of(lengths):
    lines = lengths.shape[0]
    wide = lengths.astype(F32)
    high = wide.astype(BF16)
    low = (wide - high.astype(F32)).astype(BF16)
    row = lax.broadcasted_iota(jnp.int32, (LANES, LANES), 0)
    col = lax.broadcasted_iota(jnp.int32, (LANES, LANES), 1)
    upto = jnp.where(row <= col, 1.0, 0.0).astype(BF16)
    within = dot(high, upto, 1, 0) + dot(low, upto, 1, 0)
    offset = jnp.zeros((1, 1), F32)
    ends = []
    for line in range(lines):
        ends.append(within[line : line + 1] + offset)
        offset = ends[-1][:, LANES - 1 :]
    return ends


def count_ends(ends, positions):
    count = jnp.zeros((positions.shape[0], LANES), F32)
    for line in ends:
        count = count + jnp.where(line <= positions, 1.0, 0.0)
    return jnp.sum(count, axis=1, keepdims=True)


def run_of(slot, owners):
    second = jnp.where(slot >= owners, 1, 0)
    group = slot - second * owners
    odd = lax.rem(group, 2)
    return (group - odd) * 2 + odd + second * 2


def chain_matrices(ends, run_rows, owners):
    slots = 2 * owners
    first_at = (run_of(lax.broadcasted_iota(jnp.int32, (LANES, 1), 0), owners) * run_rows).astype(F32)
    first = jnp.broadcast_to(count_ends(ends, first_at), (LANES, LANES))
    last = jnp.broadcast_to(count_ends(ends, first_at + (run_rows - 1.0)), (LANES, LANES))
    mine = run_of(lax.broadcasted_iota(jnp.int32, (LANES, LANES), 0), owners)
    other = run_of(lax.broadcasted_iota(jnp.int32, (LANES, LANES), 1), owners)
    rising = jnp.where((jnp.transpose(last) == first) & (other < mine), 1.0, 0.0)
    falling = jnp.where((jnp.transpose(first) == last) & (other > mine), 1.0, 0.0)
    return rising[:slots, :slots].astype(BF16), falling[:slots, :slots].astype(BF16)


def lanes_of(rows):
    return lax.broadcasted_iota(jnp.int32, (rows, LANES), 1)


def turn(x, by):
    by = by % LANES
    return pltpu.roll(x, by, 1) if by else x


def store_pieces(ref, sums, totals):
    owners = ref.shape[0]
    share = FEATURES // owners
    line = jnp.zeros((owners, LANES), F32)
    for i in range(share):
        part = slice(i * owners, (i + 1) * owners)
        for run in range(2):
            ref[:, run * share + i, :] = sums[run][part]
        line = line + turn(totals[part], 4 * i)
    ref[:, 2 * share, :] = line


def load_pieces(ref):
    owners = ref.shape[0]
    share = FEATURES // owners
    line = ref[:, 2 * share, :]
    totals = jnp.concatenate([turn(line, -4 * i) for i in range(share)], axis=0)
    totals = jnp.where(lanes_of(FEATURES) < 4, totals, 0.0)
    result = []
    for run in range(2):
        sums = jnp.concatenate([ref[:, run * share + i, :] for i in range(share)], axis=0)
        result.append(split2(beside(sums, totals)))
    return result


def chain(rising, falling, in_ref, out_ref):
    owners = in_ref.shape[0]
    share = FEATURES // owners
    lane = lanes_of(owners)
    second = lax.rem(lane, 4) >= 2
    blocks = []
    for i in range(share):
        blocks.append(jnp.concatenate([in_ref[:, i, :], in_ref[:, share + i, :]], axis=0))
    line = in_ref[:, 2 * share, :]
    blocks.append(
        jnp.concatenate([jnp.where(second, 0.0, line), turn(jnp.where(second, line, 0.0), -2)], axis=0)
    )
    side = lanes_of(2 * owners)
    for i, block in enumerate(blocks):
        parts = split3(block)
        up = dot(rising, parts[0], 1, 0) + dot(rising, parts[1], 1, 0) + dot(rising, parts[2], 1, 0)
        down = dot(falling, parts[0], 1, 0) + dot(falling, parts[1], 1, 0) + dot(falling, parts[2], 1, 0)
        if i < share:
            both = jnp.where(side < HEAD_DIM, up, down)
            out_ref[:, i, :] = both[:owners]
            out_ref[:, share + i, :] = both[owners:]
        else:
            both = jnp.where(lax.rem(side, 2) == 0, up, down)
            out_ref[:, 2 * share, :] = both[:owners] + turn(both[owners:], 2)


def over_peers(size, step):
    group = 7 if (size - 1) % 7 == 0 else 1

    def several(turn, carry):
        for i in range(group):
            step(turn * group + i + 1)
        return carry

    lax.fori_loop(0, (size - 1) // group, several, 0)


class Place:
    def __init__(self):
        self.wide = lax.axis_index("wide")
        self.narrow = lax.axis_index("narrow")
        self.second = lax.rem(self.wide, 2)
        self.quarter = lax.rem(self.narrow, 4)
        self.half = lax.div(self.narrow, 4)
        self.even = self.wide - self.second
        self.member = self.second * 4 + self.quarter
        self.group = self.even + self.half

    def of_member(self, member):
        quarter = lax.rem(member, 4)
        return {"wide": self.even + lax.div(member, 4), "narrow": self.half * 4 + quarter}

    def of_group(self, group):
        half = lax.rem(group, 2)
        return {"wide": group - half + self.second, "narrow": half * 4 + self.quarter}


class Exchange:
    def __init__(self, me, device_of, send, land, send_sem, recv_sem):
        self.me, self.device_of, self.size = me, device_of, send.shape[0]
        self.send, self.land, self.send_sem, self.recv_sem = send, land, send_sem, recv_sem

    def start(self):
        def step(offset):
            peer = lax.rem(self.me + offset, self.size)
            pltpu.make_async_remote_copy(
                src_ref=self.send.at[peer],
                dst_ref=self.land.at[self.me],
                send_sem=self.send_sem,
                recv_sem=self.recv_sem,
                device_id=self.device_of(peer),
                device_id_type=MESH,
            ).start()

        over_peers(self.size, step)
        self.land[self.me] = self.send[self.me]

    def all_but_one(self):
        part = pl.ds(0, self.size - 1)
        return pltpu.make_async_remote_copy(
            src_ref=self.send.at[part],
            dst_ref=self.land.at[part],
            send_sem=self.send_sem,
            recv_sem=self.recv_sem,
            device_id=self.device_of(lax.rem(self.me + 1, self.size)),
            device_id_type=MESH,
        )

    def arrived(self):
        self.all_but_one().wait_recv()

    def sent(self):
        self.all_but_one().wait_send()


def main_kernel(
    q_any, k_any, v_any, g_any, lengths_ref, proj_ref,
    first_ref, second_ref,
    q_ref, k_ref, v_ref, g_ref,
    kv_send, kv_ref, qg_send, qg_ref,
    piece, gathered, moved, state, piece_g, gathered_g, moved_g, state_g,
    done_q, back_q, done_k, back_k,
    phi_k_ref, phi_q_ref, expo_k_ref, expo_q_ref, ids_ref, a_ref, total_ref,
    score_high, score_low, coupling_high, coupling_low, key_up_ref, value_up_ref,
    in_sem, send_sem, recv_sem,
):
    fine = kv_send.shape[0]
    coarse = piece.shape[0]
    own = q_ref.shape[0]
    rows = own * fine
    run_rows = rows // 2
    strips = rows // STRIP
    blocks = STRIP // own
    here = Place()

    def within(number, send, land):
        return Exchange(here.member, here.of_member, send, land, send_sem.at[number], recv_sem.at[number])

    def across(number, send, land):
        return Exchange(here.group, here.of_group, send, land, send_sem.at[number], recv_sem.at[number])

    move_kv = within(0, kv_send, kv_ref)
    move_qg = within(1, qg_send, qg_ref)
    gather_s = across(2, piece, gathered)
    scatter_s = across(3, moved, state)
    gather_g = across(4, piece_g, gathered_g)
    scatter_g = across(5, moved_g, state_g)
    give_q = within(6, done_q, back_q)
    give_k = within(7, done_k, back_k)

    barrier = pltpu.get_barrier_semaphore()

    def greet(me, device_of, size):
        def step(offset):
            pl.semaphore_signal(
                barrier, inc=1, device_id=device_of(lax.rem(me + offset, size)), device_id_type=MESH
            )

        over_peers(size, step)

    greet(here.member, here.of_member, fine)
    greet(here.group, here.of_group, coarse)
    loads = [
        pltpu.make_async_copy(source, target, in_sem.at[i])
        for i, (source, target) in enumerate(
            ((k_any, k_ref), (v_any, v_ref), (q_any, q_ref), (g_any, g_ref))
        )
    ]
    for load in loads:
        load.start()

    def pack(left, right, target):
        for head in range(fine):
            cols = slice(head * HEAD_DIM, (head + 1) * HEAD_DIM)
            target[head] = beside(left[:, cols], right[:, cols])

    loads[0].wait()
    loads[1].wait()
    pack(k_ref, v_ref, kv_send)
    pl.semaphore_wait(barrier, fine - 1 + coarse - 1)
    move_kv.start()
    loads[2].wait()
    loads[3].wait()
    pack(q_ref, g_ref, qg_send)
    move_qg.start()

    projection = proj_ref[...]
    parts = split3(projection * INV_ROOT)
    mix_parts = jnp.concatenate([parts[0], parts[1], parts[2], jnp.zeros_like(parts[0])], axis=0)
    below = lax.broadcasted_iota(jnp.int32, projection.shape, 0) == 0
    grad_parts = split2(jnp.concatenate([projection, jnp.where(below, 1.0, 0.0)], axis=0))

    ends = ends_of(lengths_ref[...])
    rising, falling = chain_matrices(ends, run_rows, coarse)
    first_run = 2 * here.even + here.half

    class Strip:
        def __init__(self, number):
            self.at = slice(number * STRIP, (number + 1) * STRIP)
            self.slots = slice(number * blocks, (number + 1) * blocks)
            self.run = number * STRIP // run_rows
            self.whole = slice(self.run * run_rows, (self.run + 1) * run_rows)
            inside = number * STRIP - self.run * run_rows
            start = ((first_run + 2 * self.run) * run_rows + inside).astype(F32)
            self.places = lax.broadcasted_iota(jnp.int32, (STRIP, 1), 0).astype(F32) + start

        def of(self, ref):
            return ref[self.slots].reshape(STRIP, LANES)

        def sides(self):
            ids = ids_ref[self.at, :]
            ends_at = self.whole
            return ids == ids_ref[ends_at.start : ends_at.start + 1, :], ids == ids_ref[ends_at.stop - 1 : ends_at.stop, :]

        def mask(self):
            return ids_ref[self.at, :1] == id_row[:, self.whole]

        def pair(self, left, left_use, right, right_use):
            return beside(
                jnp.where(left_use[:, :HEAD_DIM], left, 0.0), jnp.where(right_use[:, :HEAD_DIM], right, 0.0)
            )

        def line(self, left_use, right_use, amount):
            lane = lanes_of(STRIP) - 2 * self.run
            use = ((lane == 0) & left_use) | ((lane == 1) & right_use)
            return jnp.where(use, jnp.broadcast_to(amount, (STRIP, LANES)), 0.0)

    every = [Strip(number) for number in range(strips)]
    for strip in every:
        ids_ref[strip.at, :] = jnp.broadcast_to(count_ends(ends, strip.places), (STRIP, LANES))
    id_row = jnp.transpose(ids_ref[...])[:1, :]
    ones = jnp.ones((STRIP, 1), F32)

    def pieces_of(phi_ref, weights):
        sums, totals = [], jnp.zeros((FEATURES, LANES), F32)
        for run in range(2):
            found = 0.0
            for strip, weight in zip(every, weights):
                if strip.run == run:
                    for part in weight:
                        found = found + dot(phi_ref[strip.at, :], part, 0, 0)
            sums.append(found[:, :LANES])
            totals = totals + found[:, LANES:]
        return sums, totals

    move_kv.arrived()
    weights = []
    for strip in every:
        packed = strip.of(kv_ref)
        expo, phi = features(packed[:, :HEAD_DIM], mix_parts)
        expo_k_ref[strip.at, :] = expo
        phi_k_ref[strip.at, :] = phi
        front, back = strip.sides()
        vectors = packed[:, HEAD_DIM:].astype(F32)
        weights.append([beside(strip.pair(vectors, back, vectors, front), strip.line(back, front, ones)).astype(BF16)])
    store_pieces(piece, *pieces_of(phi_k_ref, weights))
    gather_s.start()

    def values_of(run):
        packed = kv_ref[run * fine // 2 : (run + 1) * fine // 2].reshape(run_rows, LANES)
        return extended(packed[:, HEAD_DIM:].astype(F32), jnp.ones((run_rows, 1), F32)).astype(BF16)

    values = [values_of(run) for run in range(2)]

    move_qg.arrived()
    for strip in every:
        expo, phi = features(strip.of(qg_ref)[:, :HEAD_DIM], mix_parts)
        expo_q_ref[strip.at, :] = expo
        phi_q_ref[strip.at, :] = phi
        scores = jnp.where(strip.mask(), dot(phi, phi_k_ref[strip.whole, :], 1, 1), 0.0)
        score_high[strip.at, :], score_low[strip.at, :] = split2(scores)

    gather_s.arrived()
    chain(rising, falling, gathered, moved)
    scatter_s.start()

    for strip in every:
        total_ref[strip.at, :] = dot(score_high[strip.at, :], values[strip.run], 1, 0) + dot(
            score_low[strip.at, :], values[strip.run], 1, 0
        )

    scatter_s.arrived()
    states = load_pieces(state)
    weights = []
    for strip in every:
        front, back = strip.sides()
        phi = phi_q_ref[strip.at, :]
        grad = strip.of(qg_ref)[:, HEAD_DIM:].astype(F32)
        high, low = states[strip.run]
        far = dot(phi, high, 1, 0) + dot(phi, low, 1, 0)
        total = total_ref[strip.at, :]
        numer = total[:, :HEAD_DIM]
        numer = numer + jnp.where(front[:, :HEAD_DIM], far[:, :HEAD_DIM], 0.0)
        numer = numer + jnp.where(back[:, :HEAD_DIM], far[:, HEAD_DIM:LANES], 0.0)
        lane = LANES + 2 * strip.run
        denom = total[:, HEAD_DIM : HEAD_DIM + 1]
        denom = denom + jnp.where(front[:, :1], far[:, lane : lane + 1], 0.0)
        denom = denom + jnp.where(back[:, :1], far[:, lane + 1 : lane + 2], 0.0)
        inverse = 1.0 / denom
        attended = numer * inverse
        total_ref[strip.at, :HEAD_DIM] = attended
        bias = -jnp.sum(grad * attended, axis=1, keepdims=True) * inverse
        a = grad * inverse
        a_ref[strip.at, :] = extended(a, bias)
        weights.append(split2(beside(strip.pair(a, back, a, front), strip.line(back, front, bias))))
    store_pieces(piece_g, *pieces_of(phi_q_ref, weights))
    gather_g.start()

    for strip in every:
        front, back = strip.sides()
        a = a_ref[strip.at, :]
        bias = a[:, HEAD_DIM : HEAD_DIM + 1]
        doubled = beside(values[strip.run], values[strip.run])
        coupling = jnp.where(strip.mask(), dot(beside(*split2(a)), doubled, 1, 1), 0.0)
        high, low = split2(coupling)
        coupling_high[strip.at, :] = high
        coupling_low[strip.at, :] = low
        phi_k = phi_k_ref[strip.whole, :]
        up = dot(high, phi_k, 1, 0) + dot(low, phi_k, 1, 0)
        vectors = a[:, :HEAD_DIM]
        use_high, use_low = split2(beside(strip.pair(vectors, front, vectors, back), strip.line(front, back, bias)))
        high, low = states[strip.run]
        up = up + dot(use_high, high, 1, 1) + dot(use_high, low, 1, 1) + dot(use_low, high, 1, 1)
        query_grad = feature_grad(strip.of(qg_ref)[:, :HEAD_DIM], expo_q_ref[strip.at, :], up, grad_parts)
        done = beside(total_ref[strip.at, :HEAD_DIM], query_grad).astype(BF16)
        done_q[strip.slots] = done.reshape(blocks, own, LANES)
    give_q.start()

    gather_g.arrived()
    chain(rising, falling, gathered_g, moved_g)
    scatter_g.start()

    for run in range(2):
        whole = slice(run * run_rows, (run + 1) * run_rows)
        a_high, a_low = split2(a_ref[whole, :])
        high = score_high[whole, :]
        both = dot(beside(a_high, a_low), high, 0, 0)
        value_up_ref[:, whole] = both[:LANES] + both[LANES:] + dot(a_high, score_low[whole, :], 0, 0)
        phi = phi_q_ref[whole, :]
        key_up_ref[:, whole] = dot(phi, coupling_high[whole, :], 0, 0) + dot(phi, coupling_low[whole, :], 0, 0)

    scatter_g.arrived()
    states = load_pieces(state_g)
    for strip in every:
        front, back = strip.sides()
        phi = phi_k_ref[strip.at, :]
        packed = strip.of(kv_ref)
        vectors = packed[:, HEAD_DIM:].astype(F32)
        use = beside(strip.pair(vectors, front, vectors, back), strip.line(front, back, ones)).astype(BF16)
        high, low = states[strip.run]
        up = jnp.transpose(key_up_ref[:, strip.at]) + dot(use, high, 1, 1) + dot(use, low, 1, 1)
        far = dot(phi, high[:, :LANES], 1, 0) + dot(phi, low[:, :LANES], 1, 0)
        total = jnp.transpose(value_up_ref[:, strip.at])[:, :HEAD_DIM]
        total = total + jnp.where(front[:, :HEAD_DIM], far[:, :HEAD_DIM], 0.0)
        total = total + jnp.where(back[:, :HEAD_DIM], far[:, HEAD_DIM:], 0.0)
        key_grad = feature_grad(packed[:, :HEAD_DIM], expo_k_ref[strip.at, :], up, grad_parts)
        done_k[strip.slots] = beside(key_grad, total).astype(BF16).reshape(blocks, own, LANES)
    give_k.start()

    give_q.arrived()
    first_ref[...] = back_q[...]
    give_k.arrived()
    second_ref[...] = back_k[...]
    for each in (move_kv, move_qg, gather_s, scatter_s, gather_g, scatter_g, give_q, give_k):
        each.sent()


def body(coarse, fine, query_rows, key_rows, value_rows, out_grad, doc_lengths, projection):
    own = query_rows.shape[0]
    rows = own * fine
    shape = jax.ShapeDtypeStruct
    packed = shape((fine, own, LANES), BF16)
    lines = 2 * FEATURES // coarse + 1
    vmem = pl.BlockSpec(memory_space=pltpu.VMEM)
    anywhere = pl.BlockSpec(memory_space=pl.ANY)
    tokens = pltpu.VMEM(query_rows.shape, BF16)
    blocks = pltpu.VMEM((fine, own, LANES), BF16)
    pieces = pltpu.VMEM((coarse, lines, LANES), F32)
    narrow_rows = pltpu.VMEM((rows, LANES), BF16)
    wide_rows = pltpu.VMEM((rows, LANES), F32)
    square = pltpu.VMEM((rows, rows // 2), BF16)
    turned = pltpu.VMEM((LANES, rows), F32)
    scratch = [tokens] * 4 + [blocks] * 4 + [pieces] * 8 + [blocks] * 4
    scratch += [narrow_rows] * 2 + [wide_rows] * 5 + [square] * 4 + [turned] * 2
    scratch += [pltpu.SemaphoreType.DMA((count,)) for count in (4, 8, 8)]
    first, second = pl.pallas_call(
        main_kernel,
        out_shape=(packed, packed),
        in_specs=[anywhere] * 4 + [vmem] * 2,
        out_specs=(vmem, vmem),
        scratch_shapes=scratch,
        compiler_params=pltpu.CompilerParams(
            collective_id=0, has_side_effects=True, vmem_limit_bytes=VMEM_BYTES
        ),
        cost_estimate=pl.CostEstimate(
            flops=2 * rows * rows * LANES * 6, bytes_accessed=8 * own * fine * HEAD_DIM * 2, transcendentals=0
        ),
    )(query_rows, key_rows, value_rows, out_grad, doc_lengths.reshape(-1, LANES), projection.T)
    out = shape(query_rows.shape, BF16)
    return pl.pallas_call(
        unpack_kernel,
        out_shape=(out, out, out, out),
        in_specs=[vmem] * 2,
        out_specs=(vmem,) * 4,
        compiler_params=pltpu.CompilerParams(vmem_limit_bytes=VMEM_BYTES),
        cost_estimate=pl.CostEstimate(flops=0, bytes_accessed=8 * own * fine * HEAD_DIM * 2, transcendentals=0),
    )(first, second)


def solution(mesh):
    tokens = P(("wide", "narrow"), None)
    return jax.shard_map(
        functools.partial(body, mesh.shape["wide"], mesh.shape["narrow"]),
        mesh=mesh,
        in_specs=(tokens, tokens, tokens, tokens, P(), P()),
        out_specs=(tokens, tokens, tokens, tokens),
        check_vma=False,
    )
```

```python
import functools

import jax
import jax.numpy as jnp
from jax import lax
from jax.experimental import pallas as pl
from jax.experimental.pallas import tpu as pltpu
from jax.sharding import PartitionSpec as P

HEAD_DIM = 64
FEATURES = 128
LANES = 128
FLOOR = 1e-06
F32 = jnp.float32
BF16 = jnp.bfloat16
INV_ROOT = HEAD_DIM ** (-0.25)
FACTOR = FEATURES ** (-0.5)
VMEM_BYTES = 56 * 1024 * 1024
MESH = pl.DeviceIdType.MESH
STRIP = 256
LINE = 8


def dot(a, b, da, db):
    return lax.dot_general(a, b, (((da,), (db,)), ((), ())), preferred_element_type=F32)


def split2(x):
    high = x.astype(BF16)
    return high, (x - high.astype(F32)).astype(BF16)


def split3(x):
    high = x.astype(BF16)
    rest = x - high.astype(F32)
    mid = rest.astype(BF16)
    return high, mid, (rest - mid.astype(F32)).astype(BF16)


def beside(*parts):
    return jnp.concatenate(parts, axis=1)


def features(x, parts):
    mixed = dot(beside(x, x, x, jnp.zeros_like(x)), parts, 1, 0)
    wide = x.astype(F32)
    half = jnp.sum(wide * wide, axis=1, keepdims=True) * (0.5 * INV_ROOT * INV_ROOT)
    expo = jnp.exp(mixed - half) * FACTOR
    return expo, (expo + FLOOR * FACTOR).astype(BF16)


def extended(x, extra):
    rows = x.shape[0]
    lane = lax.broadcasted_iota(jnp.int32, (rows, HEAD_DIM), 1)
    tail = jnp.where(lane == 0, jnp.broadcast_to(extra, (rows, HEAD_DIM)), 0.0)
    return jnp.concatenate([x, tail], axis=1)


def feature_grad(x, expo, up, parts):
    high, low = split2(expo * up)
    back = dot(beside(high, low), beside(parts[0], parts[0]), 1, 1) + dot(high, parts[1], 1, 1)
    scaled = x.astype(F32) * INV_ROOT
    return (back[:, :HEAD_DIM] - scaled * back[:, HEAD_DIM : HEAD_DIM + 1]) * INV_ROOT


def unpack_kernel(first_ref, second_ref, out_a, out_b, out_c, out_d):
    for pair in range(first_ref.shape[0] // 2):
        cols = slice(pair * LANES, (pair + 1) * LANES)
        for ref, left, right in ((first_ref, out_a, out_b), (second_ref, out_c, out_d)):
            even, odd = ref[2 * pair], ref[2 * pair + 1]
            left[:, cols] = jnp.concatenate([even[:, :HEAD_DIM], odd[:, :HEAD_DIM]], axis=1)
            right[:, cols] = jnp.concatenate([even[:, HEAD_DIM:], odd[:, HEAD_DIM:]], axis=1)


def ends_of(lengths):
    lines = lengths.shape[0]
    wide = lengths.astype(F32)
    high = wide.astype(BF16)
    low = (wide - high.astype(F32)).astype(BF16)
    row = lax.broadcasted_iota(jnp.int32, (LANES, LANES), 0)
    col = lax.broadcasted_iota(jnp.int32, (LANES, LANES), 1)
    upto = jnp.where(row <= col, 1.0, 0.0).astype(BF16)
    within = dot(high, upto, 1, 0) + dot(low, upto, 1, 0)
    offset = jnp.zeros((1, 1), F32)
    ends = []
    for line in range(lines):
        ends.append(within[line : line + 1] + offset)
        offset = ends[-1][:, LANES - 1 :]
    return ends


def count_ends(ends, positions):
    count = jnp.zeros((positions.shape[0], LANES), F32)
    for line in ends:
        count = count + jnp.where(line <= positions, 1.0, 0.0)
    return jnp.sum(count, axis=1, keepdims=True)


def lanes_of(rows):
    return lax.broadcasted_iota(jnp.int32, (rows, LANES), 1)


def totals_in_rows(totals):
    return jnp.transpose(totals)[:8]


def store_pieces(ref, sums, totals):
    owners = ref.shape[0]
    share = FEATURES // owners
    for run in range(2):
        ref[:, run * share : (run + 1) * share, :] = sums[run].reshape(owners, share, LANES)
    ref[:, 2 * share :, :] = jnp.broadcast_to(totals_in_rows(totals)[None], (owners, 8, LANES))


class Chain:
    def __init__(self, ends, here, run_rows, inner, outer, row_coef, line_coef, own_coef, ids_of):
        self.inner, self.outer, self.share = inner, outer, FEATURES // inner
        self.row_coef, self.line_coef, self.own_coef = row_coef, line_coef, own_coef
        runs = 2 * inner
        size = runs + outer
        slot = lax.broadcasted_iota(jnp.int32, (size, 1), 0)
        odd = jnp.where(lax.rem(slot, 4) >= 2, 1, 0)
        of_run = here.line * runs + slot + lax.rem(slot, 2) - odd
        index = jnp.where(slot < runs, of_run, (slot - runs) * runs)
        start = (index * run_rows).astype(F32)
        length = jnp.where(slot < runs, run_rows, run_rows * runs).astype(F32)
        first = jnp.broadcast_to(count_ends(ends, start), (size, LANES))
        last = jnp.broadcast_to(count_ends(ends, start + length - 1.0), (size, LANES))
        start = jnp.broadcast_to(start, (size, LANES))
        valid = jnp.broadcast_to(slot - runs, (size, LANES)) != here.line
        left = lanes_of(size) < HEAD_DIM

        def relation(start_r, first_r, last_r):
            rising = valid & (last == first_r) & (start < start_r)
            falling = valid & (first == last_r) & (start > start_r)
            return jnp.where(rising, 1.0, 0.0), jnp.where(falling, 1.0, 0.0)

        for run in range(runs):
            at = slice(run, run + 1)
            rising, falling = relation(start[at], first[at], last[at])
            row_coef[run] = jnp.where(left, rising, falling)
        for run in range(2):
            begin = ((here.first_run + 2 * run) * run_rows).astype(F32)
            own_coef[2 * run], own_coef[2 * run + 1] = relation(begin, *ids_of(run))
        line_coef[0] = jnp.where(last == last[runs - 1 : runs], 1.0, 0.0)
        line_coef[1] = jnp.where(first == first[:1], 1.0, 0.0)
        line_coef[2] = jnp.where(left, line_coef[0], line_coef[1])

    def block(self, gathered, run):
        return gathered[run // 2, (run % 2) * self.share : (run % 2 + 1) * self.share, :]

    def total(self, gathered, run, side):
        row = 2 * self.share + 2 * (run % 2) + side
        return gathered[run // 2, row : row + 1, :]

    def sum_line(self, gathered, out):
        found = jnp.zeros((self.share, LANES), F32)
        totals = [jnp.zeros((1, LANES), F32)] * 2
        for run in range(2 * self.inner):
            found = found + self.line_coef[2, run : run + 1, :] * self.block(gathered, run)
            for side in range(2):
                totals[side] = totals[side] + self.line_coef[side, run : run + 1, :] * self.total(gathered, run, side)
        out[: self.share, :] = found
        out[self.share :, :] = jnp.concatenate(totals + [jnp.zeros((6, LANES), F32)], axis=0)

    def place(self, run):
        return run // 2, slice((run % 2) * self.share, (run % 2 + 1) * self.share)

    def from_line(self, gathered, out):
        runs = 2 * self.inner
        blocks = [self.block(gathered, run) for run in range(runs)]
        for run in range(runs):
            found = jnp.zeros((self.share, LANES), F32)
            for source in range(runs):
                if source != run:
                    found = found + self.row_coef[run, source : source + 1, :] * blocks[source]
            owner, at = self.place(run)
            out[owner, at, :] = found

    def from_lines(self, lines, out):
        runs = 2 * self.inner
        blocks = [lines[line, : self.share, :] for line in range(self.outer)]
        for run in range(runs):
            owner, at = self.place(run)
            found = out[owner, at, :]
            for line in range(self.outer):
                source = runs + line
                found = found + self.row_coef[run, source : source + 1, :] * blocks[line]
            out[owner, at, :] = found

    def totals(self, gathered, lines):
        runs = 2 * self.inner
        rows = []
        for row in range(4):
            side = row % 2
            found = jnp.zeros((1, LANES), F32)
            for source in range(runs):
                found = found + self.own_coef[row, source : source + 1, :] * self.total(gathered, source, side)
            for line in range(self.outer):
                at = self.share + side
                found = found + self.own_coef[row, runs + line : runs + line + 1, :] * lines[line, at : at + 1, :]
            rows.append(found)
        return jnp.transpose(jnp.concatenate(rows + [jnp.zeros((LANES - 4, LANES), F32)], axis=0))

    def states(self, state, totals):
        result = []
        for run in range(2):
            sums = state[:, run * self.share : (run + 1) * self.share, :].reshape(FEATURES, LANES)
            result.append(split2(beside(sums, totals)))
        return result


def over_peers(size, step):
    group = 7 if (size - 1) % 7 == 0 else 1

    def several(turn, carry):
        for i in range(group):
            step(turn * group + i + 1)
        return carry

    lax.fori_loop(0, (size - 1) // group, several, 0)


class Place:
    def __init__(self):
        self.wide = lax.axis_index("wide")
        self.narrow = lax.axis_index("narrow")
        self.second = lax.rem(self.wide, 2)
        self.quarter = lax.rem(self.narrow, 4)
        self.half = lax.div(self.narrow, 4)
        self.even = self.wide - self.second
        self.member = self.second * 4 + self.quarter
        self.line = lax.div(self.wide, LINE)
        self.base = self.line * LINE
        self.inside = self.even - self.base + self.half
        self.first_run = 2 * self.even + self.half

    def of_member(self, member):
        quarter = lax.rem(member, 4)
        return {"wide": self.even + lax.div(member, 4), "narrow": self.half * 4 + quarter}

    def of_inside(self, inside):
        half = lax.rem(inside, 2)
        return {"wide": self.base + inside - half + self.second, "narrow": half * 4 + self.quarter}

    def of_line(self, line):
        return {"wide": self.wide - self.base + line * LINE, "narrow": self.narrow}


class Exchange:
    def __init__(self, me, device_of, send, land, send_sem, recv_sem, same=False):
        self.me, self.device_of, self.size, self.same = me, device_of, land.shape[0], same
        self.send, self.land, self.send_sem, self.recv_sem = send, land, send_sem, recv_sem

    def start(self):
        def step(offset):
            peer = lax.rem(self.me + offset, self.size)
            pltpu.make_async_remote_copy(
                src_ref=self.send if self.same else self.send.at[peer],
                dst_ref=self.land.at[self.me],
                send_sem=self.send_sem,
                recv_sem=self.recv_sem,
                device_id=self.device_of(peer),
                device_id_type=MESH,
            ).start()

        over_peers(self.size, step)
        self.land[self.me] = self.send[...] if self.same else self.send[self.me]

    def all_but_one(self):
        part = self.land.at[pl.ds(0, self.size - 1)]
        return pltpu.make_async_remote_copy(
            src_ref=part,
            dst_ref=part,
            send_sem=self.send_sem,
            recv_sem=self.recv_sem,
            device_id=self.device_of(lax.rem(self.me + 1, self.size)),
            device_id_type=MESH,
        )

    def arrived(self):
        self.all_but_one().wait_recv()

    def sent(self):
        self.all_but_one().wait_send()


def main_kernel(
    q_any, k_any, v_any, g_any, lengths_ref, proj_ref,
    first_ref, second_ref,
    q_ref, k_ref, v_ref, g_ref,
    kv_send, kv_ref, qg_send, qg_ref,
    piece, gathered, line, lines, moved, state, piece_g, gathered_g, line_g, lines_g, moved_g, state_g,
    row_coef, line_coef, own_coef,
    done_q, back_q, done_k, back_k,
    phi_k_ref, phi_q_ref, expo_k_ref, expo_q_ref, ids_ref, a_ref, total_ref,
    score_high, score_low, coupling_high, coupling_low, key_up_ref, value_up_ref,
    in_sem, send_sem, recv_sem,
):
    fine = kv_send.shape[0]
    inner, outer = piece.shape[0], lines.shape[0]
    own = q_ref.shape[0]
    rows = own * fine
    run_rows = rows // 2
    strips = rows // STRIP
    blocks = STRIP // own
    here = Place()

    def within(number, send, land):
        return Exchange(here.member, here.of_member, send, land, send_sem.at[number], recv_sem.at[number])

    def across(number, send, land):
        return Exchange(here.inside, here.of_inside, send, land, send_sem.at[number], recv_sem.at[number])

    def lengthwise(number, send, land):
        return Exchange(here.line, here.of_line, send, land, send_sem.at[number], recv_sem.at[number], True)

    move_kv = within(0, kv_send, kv_ref)
    move_qg = within(1, qg_send, qg_ref)
    gather_s = across(2, piece, gathered)
    share_s = lengthwise(3, line, lines)
    scatter_s = across(4, moved, state)
    gather_g = across(5, piece_g, gathered_g)
    share_g = lengthwise(6, line_g, lines_g)
    scatter_g = across(7, moved_g, state_g)
    give_q = within(8, done_q, back_q)
    give_k = within(9, done_k, back_k)

    barrier = pltpu.get_barrier_semaphore()

    def greet(me, device_of, size):
        def step(offset):
            pl.semaphore_signal(
                barrier, inc=1, device_id=device_of(lax.rem(me + offset, size)), device_id_type=MESH
            )

        over_peers(size, step)

    greet(here.member, here.of_member, fine)
    greet(here.inside, here.of_inside, inner)
    greet(here.line, here.of_line, outer)
    loads = [
        pltpu.make_async_copy(source, target, in_sem.at[i])
        for i, (source, target) in enumerate(
            ((k_any, k_ref), (v_any, v_ref), (q_any, q_ref), (g_any, g_ref))
        )
    ]
    for load in loads:
        load.start()

    def pack(left, right, target):
        for head in range(fine):
            cols = slice(head * HEAD_DIM, (head + 1) * HEAD_DIM)
            target[head] = beside(left[:, cols], right[:, cols])

    loads[0].wait()
    loads[1].wait()
    pack(k_ref, v_ref, kv_send)
    pl.semaphore_wait(barrier, fine + inner + outer - 3)
    move_kv.start()
    loads[2].wait()
    loads[3].wait()
    pack(q_ref, g_ref, qg_send)
    move_qg.start()

    projection = proj_ref[...]
    parts = split3(projection * INV_ROOT)
    mix_parts = jnp.concatenate([parts[0], parts[1], parts[2], jnp.zeros_like(parts[0])], axis=0)
    below = lax.broadcasted_iota(jnp.int32, projection.shape, 0) == 0
    grad_parts = split2(jnp.concatenate([projection, jnp.where(below, 1.0, 0.0)], axis=0))

    ends = ends_of(lengths_ref[...])

    class Strip:
        def __init__(self, number):
            self.at = slice(number * STRIP, (number + 1) * STRIP)
            self.slots = slice(number * blocks, (number + 1) * blocks)
            self.run = number * STRIP // run_rows
            self.whole = slice(self.run * run_rows, (self.run + 1) * run_rows)
            inside = number * STRIP - self.run * run_rows
            start = ((here.first_run + 2 * self.run) * run_rows + inside).astype(F32)
            self.places = lax.broadcasted_iota(jnp.int32, (STRIP, 1), 0).astype(F32) + start

        def of(self, ref):
            return ref[self.slots].reshape(STRIP, LANES)

        def sides(self):
            ids = ids_ref[self.at, :]
            ends_at = self.whole
            return ids == ids_ref[ends_at.start : ends_at.start + 1, :], ids == ids_ref[ends_at.stop - 1 : ends_at.stop, :]

        def mask(self):
            return ids_ref[self.at, :1] == id_row[:, self.whole]

        def pair(self, left, left_use, right, right_use):
            return beside(
                jnp.where(left_use[:, :HEAD_DIM], left, 0.0), jnp.where(right_use[:, :HEAD_DIM], right, 0.0)
            )

        def line(self, left_use, right_use, amount):
            lane = lanes_of(STRIP) - 2 * self.run
            use = ((lane == 0) & left_use) | ((lane == 1) & right_use)
            return jnp.where(use, jnp.broadcast_to(amount, (STRIP, LANES)), 0.0)

    every = [Strip(number) for number in range(strips)]
    for strip in every:
        ids_ref[strip.at, :] = jnp.broadcast_to(count_ends(ends, strip.places), (STRIP, LANES))
    id_row = jnp.transpose(ids_ref[...])[:1, :]
    ones = jnp.ones((STRIP, 1), F32)

    def ids_of(run):
        begin, end = run * run_rows, (run + 1) * run_rows
        return ids_ref[begin : begin + 1, :], ids_ref[end - 1 : end, :]

    chain = Chain(ends, here, run_rows, inner, outer, row_coef, line_coef, own_coef, ids_of)

    def pieces_of(phi_ref, weights):
        sums, totals = [], jnp.zeros((FEATURES, LANES), F32)
        for run in range(2):
            found = 0.0
            for strip, weight in zip(every, weights):
                if strip.run == run:
                    for part in weight:
                        found = found + dot(phi_ref[strip.at, :], part, 0, 0)
            sums.append(found[:, :LANES])
            totals = totals + found[:, LANES:]
        return sums, totals

    move_kv.arrived()
    weights = []
    for strip in every:
        packed = strip.of(kv_ref)
        expo, phi = features(packed[:, :HEAD_DIM], mix_parts)
        expo_k_ref[strip.at, :] = expo
        phi_k_ref[strip.at, :] = phi
        front, back = strip.sides()
        vectors = packed[:, HEAD_DIM:].astype(F32)
        weights.append([beside(strip.pair(vectors, back, vectors, front), strip.line(back, front, ones)).astype(BF16)])
    store_pieces(piece, *pieces_of(phi_k_ref, weights))
    gather_s.start()

    def values_of(run):
        packed = kv_ref[run * fine // 2 : (run + 1) * fine // 2].reshape(run_rows, LANES)
        return extended(packed[:, HEAD_DIM:].astype(F32), jnp.ones((run_rows, 1), F32)).astype(BF16)

    values = [values_of(run) for run in range(2)]

    move_qg.arrived()
    for strip in every:
        expo, phi = features(strip.of(qg_ref)[:, :HEAD_DIM], mix_parts)
        expo_q_ref[strip.at, :] = expo
        phi_q_ref[strip.at, :] = phi
        scores = jnp.where(strip.mask(), dot(phi, phi_k_ref[strip.whole, :], 1, 1), 0.0)
        score_high[strip.at, :], score_low[strip.at, :] = split2(scores)

    gather_s.arrived()
    chain.sum_line(gathered, line)
    share_s.start()
    chain.from_line(gathered, moved)
    share_s.arrived()
    chain.from_lines(lines, moved)
    scatter_s.start()
    totals = chain.totals(gathered, lines)

    for strip in every:
        total_ref[strip.at, :] = dot(score_high[strip.at, :], values[strip.run], 1, 0) + dot(
            score_low[strip.at, :], values[strip.run], 1, 0
        )

    scatter_s.arrived()
    states = chain.states(state, totals)
    weights = []
    for strip in every:
        front, back = strip.sides()
        phi = phi_q_ref[strip.at, :]
        grad = strip.of(qg_ref)[:, HEAD_DIM:].astype(F32)
        high, low = states[strip.run]
        far = dot(phi, high, 1, 0) + dot(phi, low, 1, 0)
        total = total_ref[strip.at, :]
        numer = total[:, :HEAD_DIM]
        numer = numer + jnp.where(front[:, :HEAD_DIM], far[:, :HEAD_DIM], 0.0)
        numer = numer + jnp.where(back[:, :HEAD_DIM], far[:, HEAD_DIM:LANES], 0.0)
        lane = LANES + 2 * strip.run
        denom = total[:, HEAD_DIM : HEAD_DIM + 1]
        denom = denom + jnp.where(front[:, :1], far[:, lane : lane + 1], 0.0)
        denom = denom + jnp.where(back[:, :1], far[:, lane + 1 : lane + 2], 0.0)
        inverse = 1.0 / denom
        attended = numer * inverse
        total_ref[strip.at, :HEAD_DIM] = attended
        bias = -jnp.sum(grad * attended, axis=1, keepdims=True) * inverse
        a = grad * inverse
        a_ref[strip.at, :] = extended(a, bias)
        weights.append(split2(beside(strip.pair(a, back, a, front), strip.line(back, front, bias))))
    store_pieces(piece_g, *pieces_of(phi_q_ref, weights))
    gather_g.start()

    def query_part(strip):
        front, back = strip.sides()
        a = a_ref[strip.at, :]
        bias = a[:, HEAD_DIM : HEAD_DIM + 1]
        doubled = beside(values[strip.run], values[strip.run])
        coupling = jnp.where(strip.mask(), dot(beside(*split2(a)), doubled, 1, 1), 0.0)
        high, low = split2(coupling)
        coupling_high[strip.at, :] = high
        coupling_low[strip.at, :] = low
        phi_k = phi_k_ref[strip.whole, :]
        up = dot(high, phi_k, 1, 0) + dot(low, phi_k, 1, 0)
        vectors = a[:, :HEAD_DIM]
        use_high, use_low = split2(beside(strip.pair(vectors, front, vectors, back), strip.line(front, back, bias)))
        high, low = states[strip.run]
        up = up + dot(use_high, high, 1, 1) + dot(use_high, low, 1, 1) + dot(use_low, high, 1, 1)
        query_grad = feature_grad(strip.of(qg_ref)[:, :HEAD_DIM], expo_q_ref[strip.at, :], up, grad_parts)
        done = beside(total_ref[strip.at, :HEAD_DIM], query_grad).astype(BF16)
        done_q[strip.slots] = done.reshape(blocks, own, LANES)
    for strip in every[: strips // 2]:
        query_part(strip)

    gather_g.arrived()
    chain.sum_line(gathered_g, line_g)
    share_g.start()
    chain.from_line(gathered_g, moved_g)
    for strip in every[strips // 2 :]:
        query_part(strip)
    share_g.arrived()
    chain.from_lines(lines_g, moved_g)
    scatter_g.start()
    give_q.start()
    totals = chain.totals(gathered_g, lines_g)

    for run in range(2):
        whole = slice(run * run_rows, (run + 1) * run_rows)
        a_high, a_low = split2(a_ref[whole, :])
        high = score_high[whole, :]
        both = dot(beside(a_high, a_low), high, 0, 0)
        value_up_ref[:, whole] = both[:LANES] + both[LANES:] + dot(a_high, score_low[whole, :], 0, 0)
        phi = phi_q_ref[whole, :]
        key_up_ref[:, whole] = dot(phi, coupling_high[whole, :], 0, 0) + dot(phi, coupling_low[whole, :], 0, 0)

    scatter_g.arrived()
    states_g = chain.states(state_g, totals)
    for strip in every:
        front, back = strip.sides()
        phi = phi_k_ref[strip.at, :]
        packed = strip.of(kv_ref)
        vectors = packed[:, HEAD_DIM:].astype(F32)
        use = beside(strip.pair(vectors, front, vectors, back), strip.line(front, back, ones)).astype(BF16)
        high, low = states_g[strip.run]
        up = jnp.transpose(key_up_ref[:, strip.at]) + dot(use, high, 1, 1) + dot(use, low, 1, 1)
        far = dot(phi, high[:, :LANES], 1, 0) + dot(phi, low[:, :LANES], 1, 0)
        total = jnp.transpose(value_up_ref[:, strip.at])[:, :HEAD_DIM]
        total = total + jnp.where(front[:, :HEAD_DIM], far[:, :HEAD_DIM], 0.0)
        total = total + jnp.where(back[:, :HEAD_DIM], far[:, HEAD_DIM:], 0.0)
        key_grad = feature_grad(packed[:, :HEAD_DIM], expo_k_ref[strip.at, :], up, grad_parts)
        done_k[strip.slots] = beside(key_grad, total).astype(BF16).reshape(blocks, own, LANES)
    give_k.start()

    give_q.arrived()
    first_ref[...] = back_q[...]
    give_k.arrived()
    second_ref[...] = back_k[...]
    for each in (
        move_kv, move_qg, gather_s, share_s, scatter_s, gather_g, share_g, scatter_g, give_q, give_k
    ):
        each.sent()


def body(coarse, fine, query_rows, key_rows, value_rows, out_grad, doc_lengths, projection):
    own = query_rows.shape[0]
    rows = own * fine
    shape = jax.ShapeDtypeStruct
    packed = shape((fine, own, LANES), BF16)
    share = FEATURES // LINE
    outer = coarse // LINE
    sources = 2 * LINE + outer
    vmem = pl.BlockSpec(memory_space=pltpu.VMEM)
    anywhere = pl.BlockSpec(memory_space=pl.ANY)
    tokens = pltpu.VMEM(query_rows.shape, BF16)
    blocks = pltpu.VMEM((fine, own, LANES), BF16)
    pieces = pltpu.VMEM((LINE, 2 * share + 8, LANES), F32)
    results = pltpu.VMEM((LINE, 2 * share, LANES), F32)
    line_rows = share + 8
    lines = [pltpu.VMEM((line_rows, LANES), F32), pltpu.VMEM((outer, line_rows, LANES), F32)]
    phase = [pieces] * 2 + lines + [results] * 2
    coefs = [pltpu.VMEM((count, sources, LANES), F32) for count in (2 * LINE, 3, 4)]
    narrow_rows = pltpu.VMEM((rows, LANES), BF16)
    wide_rows = pltpu.VMEM((rows, LANES), F32)
    square = pltpu.VMEM((rows, rows // 2), BF16)
    turned = pltpu.VMEM((LANES, rows), F32)
    scratch = [tokens] * 4 + [blocks] * 4 + phase * 2 + coefs + [blocks] * 4
    scratch += [narrow_rows] * 2 + [wide_rows] * 5 + [square] * 4 + [turned] * 2
    scratch += [pltpu.SemaphoreType.DMA((count,)) for count in (4, 10, 10)]
    first, second = pl.pallas_call(
        main_kernel,
        out_shape=(packed, packed),
        in_specs=[anywhere] * 4 + [vmem] * 2,
        out_specs=(vmem, vmem),
        scratch_shapes=scratch,
        compiler_params=pltpu.CompilerParams(
            collective_id=0, has_side_effects=True, vmem_limit_bytes=VMEM_BYTES
        ),
        cost_estimate=pl.CostEstimate(
            flops=2 * rows * rows * LANES * 6, bytes_accessed=8 * own * fine * HEAD_DIM * 2, transcendentals=0
        ),
    )(query_rows, key_rows, value_rows, out_grad, doc_lengths.reshape(-1, LANES), projection.T)
    out = shape(query_rows.shape, BF16)
    return pl.pallas_call(
        unpack_kernel,
        out_shape=(out, out, out, out),
        in_specs=[vmem] * 2,
        out_specs=(vmem,) * 4,
        compiler_params=pltpu.CompilerParams(vmem_limit_bytes=VMEM_BYTES),
        cost_estimate=pl.CostEstimate(flops=0, bytes_accessed=8 * own * fine * HEAD_DIM * 2, transcendentals=0),
    )(first, second)


def solution(mesh):
    tokens = P(("wide", "narrow"), None)
    return jax.shard_map(
        functools.partial(body, mesh.shape["wide"], mesh.shape["narrow"]),
        mesh=mesh,
        in_specs=(tokens, tokens, tokens, tokens, P(), P()),
        out_specs=(tokens, tokens, tokens, tokens),
        check_vma=False,
    )
```

```python
import functools

import jax
import jax.numpy as jnp
from jax import lax
from jax.experimental import pallas as pl
from jax.experimental.pallas import tpu as pltpu
from jax.sharding import PartitionSpec as P

HEAD_DIM = 64
FEATURES = 128
LANES = 128
FLOOR = 1e-06
F32 = jnp.float32
BF16 = jnp.bfloat16
INV_ROOT = HEAD_DIM ** (-0.25)
FACTOR = FEATURES ** (-0.5)
VMEM_BYTES = 56 * 1024 * 1024
MESH = pl.DeviceIdType.MESH
STRIP = 256
LINE = 8


def dot(a, b, da, db):
    return lax.dot_general(a, b, (((da,), (db,)), ((), ())), preferred_element_type=F32)


def split2(x):
    high = x.astype(BF16)
    return high, (x - high.astype(F32)).astype(BF16)


def split3(x):
    high = x.astype(BF16)
    rest = x - high.astype(F32)
    mid = rest.astype(BF16)
    return high, mid, (rest - mid.astype(F32)).astype(BF16)


def beside(*parts):
    return jnp.concatenate(parts, axis=1)


def features(x, parts):
    mixed = dot(beside(x, x, x, jnp.zeros_like(x)), parts, 1, 0)
    wide = x.astype(F32)
    half = jnp.sum(wide * wide, axis=1, keepdims=True) * (0.5 * INV_ROOT * INV_ROOT)
    expo = jnp.exp(mixed - half) * FACTOR
    return expo, (expo + FLOOR * FACTOR).astype(BF16)


def extended(x, extra):
    rows = x.shape[0]
    lane = lax.broadcasted_iota(jnp.int32, (rows, HEAD_DIM), 1)
    tail = jnp.where(lane == 0, jnp.broadcast_to(extra, (rows, HEAD_DIM)), 0.0)
    return jnp.concatenate([x, tail], axis=1)


def feature_grad(x, expo, up, parts):
    high, low = split2(expo * up)
    back = dot(beside(high, low), beside(parts[0], parts[0]), 1, 1) + dot(high, parts[1], 1, 1)
    scaled = x.astype(F32) * INV_ROOT
    return (back[:, :HEAD_DIM] - scaled * back[:, HEAD_DIM : HEAD_DIM + 1]) * INV_ROOT


def unpack_kernel(first_ref, second_ref, out_a, out_b, out_c, out_d):
    for pair in range(first_ref.shape[0] // 2):
        cols = slice(pair * LANES, (pair + 1) * LANES)
        for ref, left, right in ((first_ref, out_a, out_b), (second_ref, out_c, out_d)):
            even, odd = ref[2 * pair], ref[2 * pair + 1]
            left[:, cols] = jnp.concatenate([even[:, :HEAD_DIM], odd[:, :HEAD_DIM]], axis=1)
            right[:, cols] = jnp.concatenate([even[:, HEAD_DIM:], odd[:, HEAD_DIM:]], axis=1)


def ends_of(lengths):
    lines = lengths.shape[0]
    wide = lengths.astype(F32)
    high = wide.astype(BF16)
    low = (wide - high.astype(F32)).astype(BF16)
    row = lax.broadcasted_iota(jnp.int32, (LANES, LANES), 0)
    col = lax.broadcasted_iota(jnp.int32, (LANES, LANES), 1)
    upto = jnp.where(row <= col, 1.0, 0.0).astype(BF16)
    within = dot(high, upto, 1, 0) + dot(low, upto, 1, 0)
    offset = jnp.zeros((1, 1), F32)
    ends = []
    for line in range(lines):
        ends.append(within[line : line + 1] + offset)
        offset = ends[-1][:, LANES - 1 :]
    return ends


def count_ends(ends, positions):
    count = jnp.zeros((positions.shape[0], LANES), F32)
    for line in ends:
        count = count + jnp.where(line <= positions, 1.0, 0.0)
    return jnp.sum(count, axis=1, keepdims=True)


def lanes_of(rows):
    return lax.broadcasted_iota(jnp.int32, (rows, LANES), 1)


def totals_in_rows(totals):
    return jnp.transpose(totals)[:4]


def run_of(slot, groups):
    second = jnp.where(slot >= groups, 1, 0)
    group = slot - second * groups
    odd = lax.rem(group, 2)
    return (group - odd) * 2 + odd + second * 2


def relation(own, others):
    start_r, first_r, last_r = own
    start, first, last = others
    rising = (last == first_r) & (start < start_r)
    falling = (first == last_r) & (start > start_r)
    return jnp.where(rising, 1.0, 0.0), jnp.where(falling, 1.0, 0.0)


def spans(ends, index, run_rows, length):
    start = (index * run_rows).astype(F32)
    found = (start, count_ends(ends, start), count_ends(ends, start + length - 1.0))
    return tuple(jnp.broadcast_to(x, (index.shape[0], LANES)) for x in found)


class Totals:
    def __init__(self, ends, here, run_rows, groups, coef, ids_of):
        self.groups, self.coef = groups, coef
        slot = lax.broadcasted_iota(jnp.int32, (2 * groups, 1), 0)
        others = spans(ends, run_of(slot, groups), run_rows, float(run_rows))
        for run in range(2):
            begin = ((here.first_run + 2 * run) * run_rows).astype(F32)
            coef[2 * run], coef[2 * run + 1] = relation((begin, *ids_of(run)), others)

    def collect(self, landed):
        rows = []
        sides = [jnp.concatenate([landed[:, side, :], landed[:, 2 + side, :]], axis=0) for side in range(2)]
        for row in range(4):
            rows.append(jnp.sum(self.coef[row] * sides[row % 2], axis=0, keepdims=True))
        return jnp.transpose(jnp.concatenate(rows + [jnp.zeros((LANES - 4, LANES), F32)], axis=0))


class Chain:
    def __init__(self, ends, here, run_rows, inner, outer, row_coef, line_coef):
        self.inner, self.outer, self.share = inner, outer, FEATURES // inner
        self.row_coef, self.line_coef = row_coef, line_coef
        runs = 2 * inner
        size = runs + outer
        slot = lax.broadcasted_iota(jnp.int32, (size, 1), 0)
        odd = jnp.where(lax.rem(slot, 4) >= 2, 1, 0)
        of_run = here.line * runs + slot + lax.rem(slot, 2) - odd
        index = jnp.where(slot < runs, of_run, (slot - runs) * runs)
        length = jnp.where(slot < runs, run_rows, run_rows * runs).astype(F32)
        others = spans(ends, index, run_rows, length)
        start, first, last = others
        valid = jnp.broadcast_to(slot - runs, (size, LANES)) != here.line
        left = lanes_of(size) < HEAD_DIM
        for run in range(runs):
            rising, falling = relation([x[run : run + 1] for x in others], others)
            row_coef[run] = jnp.where(valid, jnp.where(left, rising, falling), 0.0)
        ending = jnp.where(last == last[runs - 1 : runs], 1.0, 0.0)
        line_coef[...] = jnp.where(left, ending, jnp.where(first == first[:1], 1.0, 0.0))

    def block(self, gathered, run):
        return gathered[run // 2, (run % 2) * self.share : (run % 2 + 1) * self.share, :]

    def sum_line(self, gathered, out):
        found = jnp.zeros((self.share, LANES), F32)
        for run in range(2 * self.inner):
            found = found + self.line_coef[run : run + 1, :] * self.block(gathered, run)
        out[...] = found

    def place(self, run):
        return run // 2, slice((run % 2) * self.share, (run % 2 + 1) * self.share)

    def from_line(self, gathered, out):
        runs = 2 * self.inner
        blocks = [self.block(gathered, run) for run in range(runs)]
        for run in range(runs):
            found = jnp.zeros((self.share, LANES), F32)
            for source in range(runs):
                if source != run:
                    found = found + self.row_coef[run, source : source + 1, :] * blocks[source]
            owner, at = self.place(run)
            out[owner, at, :] = found

    def from_lines(self, lines, out):
        runs = 2 * self.inner
        blocks = [lines[line] for line in range(self.outer)]
        for run in range(runs):
            owner, at = self.place(run)
            found = out[owner, at, :]
            for line in range(self.outer):
                source = runs + line
                found = found + self.row_coef[run, source : source + 1, :] * blocks[line]
            out[owner, at, :] = found

    def sums(self, state):
        return [
            state[:, run * self.share : (run + 1) * self.share, :].reshape(FEATURES, LANES) for run in range(2)
        ]


def store_pieces(ref, sums):
    owners = ref.shape[0]
    share = FEATURES // owners
    for run in range(2):
        ref[:, run * share : (run + 1) * share, :] = sums[run].reshape(owners, share, LANES)


def over_peers(size, step):
    group = 7 if (size - 1) % 7 == 0 else 1

    def several(turn, carry):
        for i in range(group):
            step(turn * group + i + 1)
        return carry

    lax.fori_loop(0, (size - 1) // group, several, 0)


class Place:
    def __init__(self):
        self.wide = lax.axis_index("wide")
        self.narrow = lax.axis_index("narrow")
        self.second = lax.rem(self.wide, 2)
        self.quarter = lax.rem(self.narrow, 4)
        self.half = lax.div(self.narrow, 4)
        self.even = self.wide - self.second
        self.member = self.second * 4 + self.quarter
        self.line = lax.div(self.wide, LINE)
        self.base = self.line * LINE
        self.inside = self.even - self.base + self.half
        self.group = self.even + self.half
        self.first_run = 2 * self.even + self.half

    def of_member(self, member):
        quarter = lax.rem(member, 4)
        return {"wide": self.even + lax.div(member, 4), "narrow": self.half * 4 + quarter}

    def of_inside(self, inside):
        half = lax.rem(inside, 2)
        return {"wide": self.base + inside - half + self.second, "narrow": half * 4 + self.quarter}

    def of_group(self, group):
        half = lax.rem(group, 2)
        return {"wide": group - half + self.second, "narrow": half * 4 + self.quarter}

    def of_line(self, line):
        return {"wide": self.wide - self.base + line * LINE, "narrow": self.narrow}


class Exchange:
    def __init__(self, me, device_of, send, land, send_sem, recv_sem, same=False):
        self.me, self.device_of, self.size, self.same = me, device_of, land.shape[0], same
        self.send, self.land, self.send_sem, self.recv_sem = send, land, send_sem, recv_sem

    def start(self):
        def step(offset):
            peer = lax.rem(self.me + offset, self.size)
            pltpu.make_async_remote_copy(
                src_ref=self.send if self.same else self.send.at[peer],
                dst_ref=self.land.at[self.me],
                send_sem=self.send_sem,
                recv_sem=self.recv_sem,
                device_id=self.device_of(peer),
                device_id_type=MESH,
            ).start()

        over_peers(self.size, step)
        self.land[self.me] = self.send[...] if self.same else self.send[self.me]

    def all_but_one(self):
        part = self.land.at[pl.ds(0, self.size - 1)]
        return pltpu.make_async_remote_copy(
            src_ref=part,
            dst_ref=part,
            send_sem=self.send_sem,
            recv_sem=self.recv_sem,
            device_id=self.device_of(lax.rem(self.me + 1, self.size)),
            device_id_type=MESH,
        )

    def arrived(self):
        self.all_but_one().wait_recv()

    def sent(self):
        self.all_but_one().wait_send()


def main_kernel(
    q_any, k_any, v_any, g_any, lengths_ref, proj_ref,
    first_ref, second_ref,
    q_ref, k_ref, v_ref, g_ref,
    kv_send, kv_ref, qg_send, qg_ref,
    piece, gathered, line, lines, moved, state, piece_g, gathered_g, line_g, lines_g, moved_g, state_g,
    total_send, total_land, total_send_g, total_land_g,
    row_coef, line_coef, own_coef,
    done_q, back_q, done_k, back_k,
    phi_k_ref, phi_q_ref, expo_k_ref, expo_q_ref, ids_ref, a_ref, total_ref, inverse_ref,
    score_high, score_low, coupling_high, coupling_low, key_up_ref, value_up_ref,
    in_sem, send_sem, recv_sem,
):
    fine = kv_send.shape[0]
    inner, outer, coarse = piece.shape[0], lines.shape[0], total_land.shape[0]
    own = q_ref.shape[0]
    rows = own * fine
    run_rows = rows // 2
    strips = rows // STRIP
    blocks = STRIP // own
    here = Place()

    def within(number, send, land):
        return Exchange(here.member, here.of_member, send, land, send_sem.at[number], recv_sem.at[number])

    def across(number, send, land):
        return Exchange(here.inside, here.of_inside, send, land, send_sem.at[number], recv_sem.at[number])

    def lengthwise(number, send, land):
        return Exchange(here.line, here.of_line, send, land, send_sem.at[number], recv_sem.at[number], True)

    def everywhere(number, send, land):
        return Exchange(here.group, here.of_group, send, land, send_sem.at[number], recv_sem.at[number], True)

    move_kv = within(0, kv_send, kv_ref)
    move_qg = within(1, qg_send, qg_ref)
    gather_s = across(2, piece, gathered)
    share_s = lengthwise(3, line, lines)
    scatter_s = across(4, moved, state)
    gather_g = across(5, piece_g, gathered_g)
    share_g = lengthwise(6, line_g, lines_g)
    scatter_g = across(7, moved_g, state_g)
    give_q = within(8, done_q, back_q)
    give_k = within(9, done_k, back_k)
    tell_s = everywhere(10, total_send, total_land)
    tell_g = everywhere(11, total_send_g, total_land_g)

    barrier = pltpu.get_barrier_semaphore()

    def greet(me, device_of, size):
        def step(offset):
            pl.semaphore_signal(
                barrier, inc=1, device_id=device_of(lax.rem(me + offset, size)), device_id_type=MESH
            )

        over_peers(size, step)

    greet(here.member, here.of_member, fine)
    greet(here.group, here.of_group, coarse)
    loads = [
        pltpu.make_async_copy(source, target, in_sem.at[i])
        for i, (source, target) in enumerate(
            ((k_any, k_ref), (v_any, v_ref), (q_any, q_ref), (g_any, g_ref))
        )
    ]
    for load in loads:
        load.start()

    def pack(left, right, target):
        for head in range(fine):
            cols = slice(head * HEAD_DIM, (head + 1) * HEAD_DIM)
            target[head] = beside(left[:, cols], right[:, cols])

    loads[0].wait()
    loads[1].wait()
    pack(k_ref, v_ref, kv_send)
    pl.semaphore_wait(barrier, fine + coarse - 2)
    move_kv.start()
    loads[2].wait()
    loads[3].wait()
    pack(q_ref, g_ref, qg_send)
    move_qg.start()

    projection = proj_ref[...]
    parts = split3(projection * INV_ROOT)
    mix_parts = jnp.concatenate([parts[0], parts[1], parts[2], jnp.zeros_like(parts[0])], axis=0)
    below = lax.broadcasted_iota(jnp.int32, projection.shape, 0) == 0
    grad_parts = split2(jnp.concatenate([projection, jnp.where(below, 1.0, 0.0)], axis=0))

    ends = ends_of(lengths_ref[...])

    class Strip:
        def __init__(self, number):
            self.at = slice(number * STRIP, (number + 1) * STRIP)
            self.slots = slice(number * blocks, (number + 1) * blocks)
            self.run = number * STRIP // run_rows
            self.whole = slice(self.run * run_rows, (self.run + 1) * run_rows)
            inside = number * STRIP - self.run * run_rows
            start = ((here.first_run + 2 * self.run) * run_rows + inside).astype(F32)
            self.places = lax.broadcasted_iota(jnp.int32, (STRIP, 1), 0).astype(F32) + start

        def of(self, ref):
            return ref[self.slots].reshape(STRIP, LANES)

        def sides(self):
            ids = ids_ref[self.at, :]
            ends_at = self.whole
            return ids == ids_ref[ends_at.start : ends_at.start + 1, :], ids == ids_ref[ends_at.stop - 1 : ends_at.stop, :]

        def mask(self):
            return ids_ref[self.at, :1] == id_row[:, self.whole]

        def pair(self, left, left_use, right, right_use):
            return beside(
                jnp.where(left_use[:, :HEAD_DIM], left, 0.0), jnp.where(right_use[:, :HEAD_DIM], right, 0.0)
            )

        def line(self, left_use, right_use, amount):
            lane = lanes_of(STRIP) - 2 * self.run
            use = ((lane == 0) & left_use) | ((lane == 1) & right_use)
            return jnp.where(use, jnp.broadcast_to(amount, (STRIP, LANES)), 0.0)

    every = [Strip(number) for number in range(strips)]
    for strip in every:
        ids_ref[strip.at, :] = jnp.broadcast_to(count_ends(ends, strip.places), (STRIP, LANES))
    id_row = jnp.transpose(ids_ref[...])[:1, :]
    ones = jnp.ones((STRIP, 1), F32)

    def ids_of(run):
        begin, end = run * run_rows, (run + 1) * run_rows
        return ids_ref[begin : begin + 1, :], ids_ref[end - 1 : end, :]

    chain = Chain(ends, here, run_rows, inner, outer, row_coef, line_coef)
    collector = Totals(ends, here, run_rows, coarse, own_coef, ids_of)

    def pieces_of(phi_ref, weights):
        result = []
        for run in range(2):
            found = 0.0
            for strip, weight in zip(every, weights):
                if strip.run == run:
                    for part in weight:
                        found = found + dot(phi_ref[strip.at, :], part, 0, 0)
            result.append(found)
        return result

    move_kv.arrived()
    weights = []
    for strip in every:
        packed = strip.of(kv_ref)
        expo, phi = features(packed[:, :HEAD_DIM], mix_parts)
        expo_k_ref[strip.at, :] = expo
        phi_k_ref[strip.at, :] = phi
        front, back = strip.sides()
        vectors = packed[:, HEAD_DIM:].astype(F32)
        weights.append([beside(strip.pair(vectors, back, vectors, front), strip.line(back, front, ones)).astype(BF16)])
    found = pieces_of(phi_k_ref, weights)
    store_pieces(piece, [x[:, :LANES] for x in found])
    gather_s.start()
    total_send[...] = totals_in_rows(found[0][:, LANES:] + found[1][:, LANES:])
    tell_s.start()

    def values_of(run):
        packed = kv_ref[run * fine // 2 : (run + 1) * fine // 2].reshape(run_rows, LANES)
        return extended(packed[:, HEAD_DIM:].astype(F32), jnp.ones((run_rows, 1), F32)).astype(BF16)

    values = [values_of(run) for run in range(2)]

    move_qg.arrived()
    for strip in every:
        expo, phi = features(strip.of(qg_ref)[:, :HEAD_DIM], mix_parts)
        expo_q_ref[strip.at, :] = expo
        phi_q_ref[strip.at, :] = phi
        scores = jnp.where(strip.mask(), dot(phi, phi_k_ref[strip.whole, :], 1, 1), 0.0)
        score_high[strip.at, :], score_low[strip.at, :] = split2(scores)

    gather_s.arrived()
    chain.sum_line(gathered, line)
    share_s.start()
    chain.from_line(gathered, moved)

    for strip in every:
        total_ref[strip.at, :] = dot(score_high[strip.at, :], values[strip.run], 1, 0) + dot(
            score_low[strip.at, :], values[strip.run], 1, 0
        )

    tell_s.arrived()
    totals = collector.collect(total_land)
    totals_high, totals_low = split2(totals)
    weights = []
    for strip in every:
        front, back = strip.sides()
        phi = phi_q_ref[strip.at, :]
        grad = strip.of(qg_ref)[:, HEAD_DIM:].astype(F32)
        far = dot(phi, totals_high, 1, 0) + dot(phi, totals_low, 1, 0)
        lane = 2 * strip.run
        denom = total_ref[strip.at, HEAD_DIM : HEAD_DIM + 1]
        denom = denom + jnp.where(front[:, :1], far[:, lane : lane + 1], 0.0)
        denom = denom + jnp.where(back[:, :1], far[:, lane + 1 : lane + 2], 0.0)
        inverse = 1.0 / denom
        inverse_ref[strip.at, :] = jnp.broadcast_to(inverse, (STRIP, LANES))
        a = grad * inverse
        a_ref[strip.at, :] = extended(a, jnp.zeros((STRIP, 1), F32))
        weights.append(split2(strip.pair(a, back, a, front)))
    store_pieces(piece_g, pieces_of(phi_q_ref, weights))
    gather_g.start()

    share_s.arrived()
    chain.from_lines(lines, moved)
    scatter_s.start()

    for run in range(2):
        whole = slice(run * run_rows, (run + 1) * run_rows)
        a_high, a_low = split2(a_ref[whole, :])
        both = dot(beside(a_high, a_low), score_high[whole, :], 0, 0)
        value_up_ref[:, whole] = both[:LANES] + both[LANES:] + dot(a_high, score_low[whole, :], 0, 0)

    gather_g.arrived()
    chain.sum_line(gathered_g, line_g)
    share_g.start()
    chain.from_line(gathered_g, moved_g)

    scatter_s.arrived()
    states = [split2(beside(sums, totals)) for sums in chain.sums(state)]
    weights = []
    for strip in every:
        front, back = strip.sides()
        phi = phi_q_ref[strip.at, :]
        grad = strip.of(qg_ref)[:, HEAD_DIM:].astype(F32)
        high, low = states[strip.run]
        far = dot(phi, high[:, :LANES], 1, 0) + dot(phi, low[:, :LANES], 1, 0)
        numer = total_ref[strip.at, :HEAD_DIM]
        numer = numer + jnp.where(front[:, :HEAD_DIM], far[:, :HEAD_DIM], 0.0)
        numer = numer + jnp.where(back[:, :HEAD_DIM], far[:, HEAD_DIM:], 0.0)
        inverse = inverse_ref[strip.at, :HEAD_DIM]
        attended = numer * inverse
        total_ref[strip.at, :HEAD_DIM] = attended
        bias = -jnp.sum(grad * attended, axis=1, keepdims=True) * inverse[:, :1]
        a_ref[strip.at, :] = extended(a_ref[strip.at, :HEAD_DIM], bias)
        weights.append(split2(strip.line(back, front, bias)))
    found = pieces_of(phi_q_ref, weights)
    total_send_g[...] = totals_in_rows(found[0] + found[1])
    tell_g.start()

    def query_part(strip):
        front, back = strip.sides()
        a = a_ref[strip.at, :]
        bias = a[:, HEAD_DIM : HEAD_DIM + 1]
        doubled = beside(values[strip.run], values[strip.run])
        coupling = jnp.where(strip.mask(), dot(beside(*split2(a)), doubled, 1, 1), 0.0)
        high, low = split2(coupling)
        coupling_high[strip.at, :] = high
        coupling_low[strip.at, :] = low
        phi_k = phi_k_ref[strip.whole, :]
        up = dot(high, phi_k, 1, 0) + dot(low, phi_k, 1, 0)
        vectors = a[:, :HEAD_DIM]
        use_high, use_low = split2(beside(strip.pair(vectors, front, vectors, back), strip.line(front, back, bias)))
        high, low = states[strip.run]
        up = up + dot(use_high, high, 1, 1) + dot(use_high, low, 1, 1) + dot(use_low, high, 1, 1)
        query_grad = feature_grad(strip.of(qg_ref)[:, :HEAD_DIM], expo_q_ref[strip.at, :], up, grad_parts)
        done = beside(total_ref[strip.at, :HEAD_DIM], query_grad).astype(BF16)
        done_q[strip.slots] = done.reshape(blocks, own, LANES)
    for strip in every[: strips // 2]:
        query_part(strip)

    share_g.arrived()
    chain.from_lines(lines_g, moved_g)
    scatter_g.start()

    for strip in every[strips // 2 :]:
        query_part(strip)
    give_q.start()

    for run in range(2):
        whole = slice(run * run_rows, (run + 1) * run_rows)
        phi = phi_q_ref[whole, :]
        key_up_ref[:, whole] = dot(phi, coupling_high[whole, :], 0, 0) + dot(phi, coupling_low[whole, :], 0, 0)

    scatter_g.arrived()
    tell_g.arrived()
    totals_g = collector.collect(total_land_g)
    states_g = [split2(beside(sums, totals_g)) for sums in chain.sums(state_g)]
    for strip in every:
        front, back = strip.sides()
        phi = phi_k_ref[strip.at, :]
        packed = strip.of(kv_ref)
        vectors = packed[:, HEAD_DIM:].astype(F32)
        use = beside(strip.pair(vectors, front, vectors, back), strip.line(front, back, ones)).astype(BF16)
        high, low = states_g[strip.run]
        up = jnp.transpose(key_up_ref[:, strip.at]) + dot(use, high, 1, 1) + dot(use, low, 1, 1)
        far = dot(phi, high[:, :LANES], 1, 0) + dot(phi, low[:, :LANES], 1, 0)
        total = jnp.transpose(value_up_ref[:, strip.at])[:, :HEAD_DIM]
        total = total + jnp.where(front[:, :HEAD_DIM], far[:, :HEAD_DIM], 0.0)
        total = total + jnp.where(back[:, :HEAD_DIM], far[:, HEAD_DIM:], 0.0)
        key_grad = feature_grad(packed[:, :HEAD_DIM], expo_k_ref[strip.at, :], up, grad_parts)
        done_k[strip.slots] = beside(key_grad, total).astype(BF16).reshape(blocks, own, LANES)
    give_k.start()

    give_q.arrived()
    first_ref[...] = back_q[...]
    give_k.arrived()
    second_ref[...] = back_k[...]
    for each in (
        move_kv, move_qg, gather_s, share_s, scatter_s, gather_g, share_g, scatter_g, give_q, give_k, tell_s, tell_g
    ):
        each.sent()


def body(coarse, fine, query_rows, key_rows, value_rows, out_grad, doc_lengths, projection):
    own = query_rows.shape[0]
    rows = own * fine
    shape = jax.ShapeDtypeStruct
    packed = shape((fine, own, LANES), BF16)
    share = FEATURES // LINE
    outer = coarse // LINE
    sources = 2 * LINE + outer
    vmem = pl.BlockSpec(memory_space=pltpu.VMEM)
    anywhere = pl.BlockSpec(memory_space=pl.ANY)
    tokens = pltpu.VMEM(query_rows.shape, BF16)
    blocks = pltpu.VMEM((fine, own, LANES), BF16)
    pieces = pltpu.VMEM((LINE, 2 * share, LANES), F32)
    results = pltpu.VMEM((LINE, 2 * share, LANES), F32)
    lines = [pltpu.VMEM((share, LANES), F32), pltpu.VMEM((outer, share, LANES), F32)]
    told = [pltpu.VMEM((4, LANES), F32), pltpu.VMEM((coarse, 4, LANES), F32)]
    phase = [pieces] * 2 + lines + [results] * 2
    coefs = [pltpu.VMEM(x + (LANES,), F32) for x in ((2 * LINE, sources), (sources,), (4, 2 * coarse))]
    narrow_rows = pltpu.VMEM((rows, LANES), BF16)
    wide_rows = pltpu.VMEM((rows, LANES), F32)
    square = pltpu.VMEM((rows, rows // 2), BF16)
    turned = pltpu.VMEM((LANES, rows), F32)
    scratch = [tokens] * 4 + [blocks] * 4 + phase * 2 + told * 2 + coefs + [blocks] * 4
    scratch += [narrow_rows] * 2 + [wide_rows] * 6 + [square] * 4 + [turned] * 2
    scratch += [pltpu.SemaphoreType.DMA((count,)) for count in (4, 12, 12)]
    first, second = pl.pallas_call(
        main_kernel,
        out_shape=(packed, packed),
        in_specs=[anywhere] * 4 + [vmem] * 2,
        out_specs=(vmem, vmem),
        scratch_shapes=scratch,
        compiler_params=pltpu.CompilerParams(
            collective_id=0, has_side_effects=True, vmem_limit_bytes=VMEM_BYTES
        ),
        cost_estimate=pl.CostEstimate(
            flops=2 * rows * rows * LANES * 6, bytes_accessed=8 * own * fine * HEAD_DIM * 2, transcendentals=0
        ),
    )(query_rows, key_rows, value_rows, out_grad, doc_lengths.reshape(-1, LANES), projection.T)
    out = shape(query_rows.shape, BF16)
    return pl.pallas_call(
        unpack_kernel,
        out_shape=(out, out, out, out),
        in_specs=[vmem] * 2,
        out_specs=(vmem,) * 4,
        compiler_params=pltpu.CompilerParams(vmem_limit_bytes=VMEM_BYTES),
        cost_estimate=pl.CostEstimate(flops=0, bytes_accessed=8 * own * fine * HEAD_DIM * 2, transcendentals=0),
    )(first, second)


def solution(mesh):
    tokens = P(("wide", "narrow"), None)
    return jax.shard_map(
        functools.partial(body, mesh.shape["wide"], mesh.shape["narrow"]),
        mesh=mesh,
        in_specs=(tokens, tokens, tokens, tokens, P(), P()),
        out_specs=(tokens, tokens, tokens, tokens),
        check_vma=False,
    )
```

```python
import functools

import jax
import jax.numpy as jnp
from jax import lax
from jax.experimental import pallas as pl
from jax.experimental.pallas import tpu as pltpu
from jax.sharding import PartitionSpec as P

HEAD_DIM = 64
FEATURES = 128
LANES = 128
FLOOR = 1e-06
F32 = jnp.float32
BF16 = jnp.bfloat16
INV_ROOT = HEAD_DIM ** (-0.25)
FACTOR = FEATURES ** (-0.5)
VMEM_BYTES = 56 * 1024 * 1024
MESH = pl.DeviceIdType.MESH
STRIP = 256
LINE = 8


def dot(a, b, da, db):
    return lax.dot_general(a, b, (((da,), (db,)), ((), ())), preferred_element_type=F32)


def split2(x):
    high = x.astype(BF16)
    return high, (x - high.astype(F32)).astype(BF16)


def split3(x):
    high = x.astype(BF16)
    rest = x - high.astype(F32)
    mid = rest.astype(BF16)
    return high, mid, (rest - mid.astype(F32)).astype(BF16)


def beside(*parts):
    return jnp.concatenate(parts, axis=1)


def features(x, parts):
    mixed = dot(beside(x, x, x, jnp.zeros_like(x)), parts, 1, 0)
    wide = x.astype(F32)
    half = jnp.sum(wide * wide, axis=1, keepdims=True) * (0.5 * INV_ROOT * INV_ROOT)
    expo = jnp.exp(mixed - half) * FACTOR
    return expo, (expo + FLOOR * FACTOR).astype(BF16)


def extended(x, extra):
    rows = x.shape[0]
    lane = lax.broadcasted_iota(jnp.int32, (rows, HEAD_DIM), 1)
    tail = jnp.where(lane == 0, jnp.broadcast_to(extra, (rows, HEAD_DIM)), 0.0)
    return jnp.concatenate([x, tail], axis=1)


def feature_grad(x, expo, up, parts):
    high, low = split2(expo * up)
    back = dot(beside(high, low), beside(parts[0], parts[0]), 1, 1) + dot(high, parts[1], 1, 1)
    scaled = x.astype(F32) * INV_ROOT
    return (back[:, :HEAD_DIM] - scaled * back[:, HEAD_DIM : HEAD_DIM + 1]) * INV_ROOT


def unpack_kernel(first_ref, second_ref, out_a, out_b, out_c, out_d):
    for pair in range(first_ref.shape[0] // 2):
        cols = slice(pair * LANES, (pair + 1) * LANES)
        for ref, left, right in ((first_ref, out_a, out_b), (second_ref, out_c, out_d)):
            even, odd = ref[2 * pair], ref[2 * pair + 1]
            left[:, cols] = jnp.concatenate([even[:, :HEAD_DIM], odd[:, :HEAD_DIM]], axis=1)
            right[:, cols] = jnp.concatenate([even[:, HEAD_DIM:], odd[:, HEAD_DIM:]], axis=1)


def ends_of(lengths):
    lines = lengths.shape[0]
    wide = lengths.astype(F32)
    high = wide.astype(BF16)
    low = (wide - high.astype(F32)).astype(BF16)
    row = lax.broadcasted_iota(jnp.int32, (LANES, LANES), 0)
    col = lax.broadcasted_iota(jnp.int32, (LANES, LANES), 1)
    upto = jnp.where(row <= col, 1.0, 0.0).astype(BF16)
    within = dot(high, upto, 1, 0) + dot(low, upto, 1, 0)
    offset = jnp.zeros((1, 1), F32)
    ends = []
    for line in range(lines):
        ends.append(within[line : line + 1] + offset)
        offset = ends[-1][:, LANES - 1 :]
    return ends


def count_ends(ends, positions):
    count = jnp.zeros((positions.shape[0], LANES), F32)
    for line in ends:
        count = count + jnp.where(line <= positions, 1.0, 0.0)
    return jnp.sum(count, axis=1, keepdims=True)


def lanes_of(rows):
    return lax.broadcasted_iota(jnp.int32, (rows, LANES), 1)


def totals_in_rows(totals):
    return jnp.transpose(totals)[:4]


def run_of(slot, groups):
    second = jnp.where(slot >= groups, 1, 0)
    group = slot - second * groups
    odd = lax.rem(group, 2)
    return (group - odd) * 2 + odd + second * 2


def relation(own, others):
    start_r, first_r, last_r = own
    start, first, last = others
    rising = (last == first_r) & (start < start_r)
    falling = (first == last_r) & (start > start_r)
    return jnp.where(rising, 1.0, 0.0), jnp.where(falling, 1.0, 0.0)


def spans(ends, index, run_rows, length):
    start = (index * run_rows).astype(F32)
    found = (start, count_ends(ends, start), count_ends(ends, start + length - 1.0))
    return tuple(jnp.broadcast_to(x, (index.shape[0], LANES)) for x in found)


class Totals:
    def __init__(self, ends, here, run_rows, groups, coef, ids_of):
        self.groups, self.coef = groups, coef
        slot = lax.broadcasted_iota(jnp.int32, (2 * groups, 1), 0)
        others = spans(ends, run_of(slot, groups), run_rows, float(run_rows))
        for run in range(2):
            begin = ((here.first_run + 2 * run) * run_rows).astype(F32)
            coef[2 * run], coef[2 * run + 1] = relation((begin, *ids_of(run)), others)

    def collect(self, landed):
        rows = []
        sides = [jnp.concatenate([landed[:, side, :], landed[:, 2 + side, :]], axis=0) for side in range(2)]
        for row in range(4):
            rows.append(jnp.sum(self.coef[row] * sides[row % 2], axis=0, keepdims=True))
        return jnp.transpose(jnp.concatenate(rows + [jnp.zeros((LANES - 4, LANES), F32)], axis=0))


class Chain:
    def __init__(self, ends, here, run_rows, inner, outer, row_coef, line_coef):
        self.inner, self.outer, self.share = inner, outer, FEATURES // inner
        self.row_coef, self.line_coef = row_coef, line_coef
        runs = 2 * inner
        size = runs + outer
        slot = lax.broadcasted_iota(jnp.int32, (size, 1), 0)
        odd = jnp.where(lax.rem(slot, 4) >= 2, 1, 0)
        of_run = here.line * runs + slot + lax.rem(slot, 2) - odd
        index = jnp.where(slot < runs, of_run, (slot - runs) * runs)
        length = jnp.where(slot < runs, run_rows, run_rows * runs).astype(F32)
        others = spans(ends, index, run_rows, length)
        start, first, last = others
        valid = jnp.broadcast_to(slot - runs, (size, LANES)) != here.line
        left = lanes_of(size) < HEAD_DIM
        for run in range(runs):
            rising, falling = relation([x[run : run + 1] for x in others], others)
            row_coef[run] = jnp.where(valid, jnp.where(left, rising, falling), 0.0)
        ending = jnp.where(last == last[runs - 1 : runs], 1.0, 0.0)
        line_coef[...] = jnp.where(left, ending, jnp.where(first == first[:1], 1.0, 0.0))

    def block(self, gathered, run):
        return gathered[run // 2, (run % 2) * self.share : (run % 2 + 1) * self.share, :]

    def sum_line(self, gathered, out):
        found = jnp.zeros((self.share, LANES), F32)
        for run in range(2 * self.inner):
            found = found + self.line_coef[run : run + 1, :] * self.block(gathered, run)
        out[...] = found

    def place(self, run):
        return run // 2, slice((run % 2) * self.share, (run % 2 + 1) * self.share)

    def from_line(self, gathered, out):
        runs = 2 * self.inner
        blocks = [self.block(gathered, run) for run in range(runs)]
        for run in range(runs):
            found = jnp.zeros((self.share, LANES), F32)
            for source in range(runs):
                if source != run:
                    found = found + self.row_coef[run, source : source + 1, :] * blocks[source]
            owner, at = self.place(run)
            out[owner, at, :] = found

    def from_lines(self, lines, out):
        runs = 2 * self.inner
        blocks = [lines[line] for line in range(self.outer)]
        for run in range(runs):
            owner, at = self.place(run)
            found = out[owner, at, :]
            for line in range(self.outer):
                source = runs + line
                found = found + self.row_coef[run, source : source + 1, :] * blocks[line]
            out[owner, at, :] = found

    def sums(self, state):
        return [
            state[:, run * self.share : (run + 1) * self.share, :].reshape(FEATURES, LANES) for run in range(2)
        ]


def store_pieces(ref, sums):
    owners = ref.shape[0]
    share = FEATURES // owners
    for run in range(2):
        ref[:, run * share : (run + 1) * share, :] = sums[run].reshape(owners, share, LANES)


def over_peers(size, step):
    group = 7 if (size - 1) % 7 == 0 else 1

    def several(turn, carry):
        for i in range(group):
            step(turn * group + i + 1)
        return carry

    lax.fori_loop(0, (size - 1) // group, several, 0)


class Place:
    def __init__(self):
        self.wide = lax.axis_index("wide")
        self.narrow = lax.axis_index("narrow")
        self.second = lax.rem(self.wide, 2)
        self.quarter = lax.rem(self.narrow, 4)
        self.half = lax.div(self.narrow, 4)
        self.even = self.wide - self.second
        self.member = self.second * 4 + self.quarter
        self.line = lax.div(self.wide, LINE)
        self.base = self.line * LINE
        self.inside = self.even - self.base + self.half
        self.group = self.even + self.half
        self.first_run = 2 * self.even + self.half

    def of_member(self, member):
        quarter = lax.rem(member, 4)
        return {"wide": self.even + lax.div(member, 4), "narrow": self.half * 4 + quarter}

    def of_inside(self, inside):
        half = lax.rem(inside, 2)
        return {"wide": self.base + inside - half + self.second, "narrow": half * 4 + self.quarter}

    def of_group(self, group):
        half = lax.rem(group, 2)
        return {"wide": group - half + self.second, "narrow": half * 4 + self.quarter}

    def of_line(self, line):
        return {"wide": self.wide - self.base + line * LINE, "narrow": self.narrow}


class Exchange:
    def __init__(self, me, device_of, send, land, send_sem, recv_sem, same=False):
        self.me, self.device_of, self.size, self.same = me, device_of, land.shape[0], same
        self.send, self.land, self.send_sem, self.recv_sem = send, land, send_sem, recv_sem

    def start(self):
        def step(offset):
            peer = lax.rem(self.me + offset, self.size)
            pltpu.make_async_remote_copy(
                src_ref=self.send if self.same else self.send.at[peer],
                dst_ref=self.land.at[self.me],
                send_sem=self.send_sem,
                recv_sem=self.recv_sem,
                device_id=self.device_of(peer),
                device_id_type=MESH,
            ).start()

        over_peers(self.size, step)
        self.land[self.me] = self.send[...] if self.same else self.send[self.me]

    def all_but_one(self):
        part = self.land.at[pl.ds(0, self.size - 1)]
        return pltpu.make_async_remote_copy(
            src_ref=part,
            dst_ref=part,
            send_sem=self.send_sem,
            recv_sem=self.recv_sem,
            device_id=self.device_of(lax.rem(self.me + 1, self.size)),
            device_id_type=MESH,
        )

    def arrived(self):
        self.all_but_one().wait_recv()

    def sent(self):
        self.all_but_one().wait_send()


def main_kernel(
    q_any, k_any, v_any, g_any, lengths_ref, proj_ref,
    first_ref, second_ref,
    q_ref, k_ref, v_ref, g_ref,
    kv_send, kv_ref, qg_send, qg_ref,
    piece, gathered, line, lines, moved, state, piece_g, gathered_g, line_g, lines_g, moved_g, state_g,
    total_send, total_land, total_send_g, total_land_g,
    row_coef, line_coef, own_coef,
    done_q, back_q, done_k, back_k,
    phi_k_ref, phi_q_ref, expo_k_ref, expo_q_ref, ids_ref, a_ref, total_ref, inverse_ref,
    score_high, score_low, coupling_high, coupling_low, key_up_ref, value_up_ref,
    in_sem, send_sem, recv_sem, line_sem,
):
    fine = kv_send.shape[0]
    inner, outer, coarse = piece.shape[0], lines.shape[0], total_land.shape[0]
    own = q_ref.shape[0]
    rows = own * fine
    run_rows = rows // 2
    strips = rows // STRIP
    blocks = STRIP // own
    here = Place()

    def within(number, send, land):
        return Exchange(here.member, here.of_member, send, land, send_sem.at[number], recv_sem.at[number])

    def across(number, send, land):
        return Exchange(here.inside, here.of_inside, send, land, send_sem.at[number], recv_sem.at[number])

    def lengthwise(number, send, land):
        return Exchange(here.line, here.of_line, send, land, send_sem.at[number], recv_sem.at[number], True)

    def everywhere(number, send, land):
        return Exchange(here.group, here.of_group, send, land, send_sem.at[number], recv_sem.at[number], True)

    move_kv = within(0, kv_send, kv_ref)
    move_qg = within(1, qg_send, qg_ref)
    gather_s = across(2, piece, gathered)
    share_s = lengthwise(3, line, lines)
    scatter_s = across(4, moved, state)
    gather_g = across(5, piece_g, gathered_g)
    share_g = lengthwise(6, line_g, lines_g)
    scatter_g = across(7, moved_g, state_g)
    give_q = within(8, done_q, back_q)
    give_k = within(9, done_k, back_k)
    tell_s = everywhere(10, total_send, total_land)
    tell_g = everywhere(11, total_send_g, total_land_g)

    barrier = pltpu.get_barrier_semaphore()

    def greet(sem, me, device_of, size):
        def step(offset):
            pl.semaphore_signal(
                sem, inc=1, device_id=device_of(lax.rem(me + offset, size)), device_id_type=MESH
            )

        over_peers(size, step)

    loads = [
        pltpu.make_async_copy(source, target, in_sem.at[i])
        for i, (source, target) in enumerate(
            ((k_any, k_ref), (v_any, v_ref), (q_any, q_ref), (g_any, g_ref))
        )
    ]
    for load in loads:
        load.start()
    greet(barrier, here.member, here.of_member, fine)
    greet(barrier, here.inside, here.of_inside, inner)
    greet(barrier, here.line, here.of_line, outer)

    def pack(left, right, target):
        for head in range(fine):
            cols = slice(head * HEAD_DIM, (head + 1) * HEAD_DIM)
            target[head] = beside(left[:, cols], right[:, cols])

    loads[0].wait()
    loads[1].wait()
    pack(k_ref, v_ref, kv_send)
    pl.semaphore_wait(barrier, fine + inner + outer - 3)
    move_kv.start()
    greet(line_sem, here.line, here.of_line, outer)
    loads[2].wait()
    loads[3].wait()
    pack(q_ref, g_ref, qg_send)
    move_qg.start()

    projection = proj_ref[...]
    parts = split3(projection * INV_ROOT)
    mix_parts = jnp.concatenate([parts[0], parts[1], parts[2], jnp.zeros_like(parts[0])], axis=0)
    below = lax.broadcasted_iota(jnp.int32, projection.shape, 0) == 0
    grad_parts = split2(jnp.concatenate([projection, jnp.where(below, 1.0, 0.0)], axis=0))

    ends = ends_of(lengths_ref[...])

    class Strip:
        def __init__(self, number):
            self.at = slice(number * STRIP, (number + 1) * STRIP)
            self.slots = slice(number * blocks, (number + 1) * blocks)
            self.run = number * STRIP // run_rows
            self.whole = slice(self.run * run_rows, (self.run + 1) * run_rows)
            inside = number * STRIP - self.run * run_rows
            start = ((here.first_run + 2 * self.run) * run_rows + inside).astype(F32)
            self.places = lax.broadcasted_iota(jnp.int32, (STRIP, 1), 0).astype(F32) + start

        def of(self, ref):
            return ref[self.slots].reshape(STRIP, LANES)

        def sides(self):
            ids = ids_ref[self.at, :]
            ends_at = self.whole
            return ids == ids_ref[ends_at.start : ends_at.start + 1, :], ids == ids_ref[ends_at.stop - 1 : ends_at.stop, :]

        def mask(self):
            return ids_ref[self.at, :1] == id_row[:, self.whole]

        def pair(self, left, left_use, right, right_use):
            return beside(
                jnp.where(left_use[:, :HEAD_DIM], left, 0.0), jnp.where(right_use[:, :HEAD_DIM], right, 0.0)
            )

        def line(self, left_use, right_use, amount):
            lane = lanes_of(STRIP) - 2 * self.run
            use = ((lane == 0) & left_use) | ((lane == 1) & right_use)
            return jnp.where(use, jnp.broadcast_to(amount, (STRIP, LANES)), 0.0)

    every = [Strip(number) for number in range(strips)]
    for strip in every:
        ids_ref[strip.at, :] = jnp.broadcast_to(count_ends(ends, strip.places), (STRIP, LANES))
    id_row = jnp.transpose(ids_ref[...])[:1, :]
    ones = jnp.ones((STRIP, 1), F32)

    def ids_of(run):
        begin, end = run * run_rows, (run + 1) * run_rows
        return ids_ref[begin : begin + 1, :], ids_ref[end - 1 : end, :]

    chain = Chain(ends, here, run_rows, inner, outer, row_coef, line_coef)
    collector = Totals(ends, here, run_rows, coarse, own_coef, ids_of)

    def pieces_of(phi_ref, weights):
        result = []
        for run in range(2):
            found = 0.0
            for strip, weight in zip(every, weights):
                if strip.run == run:
                    for part in weight:
                        found = found + dot(phi_ref[strip.at, :], part, 0, 0)
            result.append(found)
        return result

    move_kv.arrived()
    weights = []
    for strip in every:
        packed = strip.of(kv_ref)
        expo, phi = features(packed[:, :HEAD_DIM], mix_parts)
        expo_k_ref[strip.at, :] = expo
        phi_k_ref[strip.at, :] = phi
        front, back = strip.sides()
        vectors = packed[:, HEAD_DIM:].astype(F32)
        weights.append([beside(strip.pair(vectors, back, vectors, front), strip.line(back, front, ones)).astype(BF16)])
    found = pieces_of(phi_k_ref, weights)
    store_pieces(piece, [x[:, :LANES] for x in found])
    gather_s.start()
    total_send[...] = totals_in_rows(found[0][:, LANES:] + found[1][:, LANES:])
    pl.semaphore_wait(line_sem, outer - 1)
    tell_s.start()

    def values_of(run):
        packed = kv_ref[run * fine // 2 : (run + 1) * fine // 2].reshape(run_rows, LANES)
        return extended(packed[:, HEAD_DIM:].astype(F32), jnp.ones((run_rows, 1), F32)).astype(BF16)

    values = [values_of(run) for run in range(2)]

    move_qg.arrived()
    for strip in every:
        expo, phi = features(strip.of(qg_ref)[:, :HEAD_DIM], mix_parts)
        expo_q_ref[strip.at, :] = expo
        phi_q_ref[strip.at, :] = phi
        scores = jnp.where(strip.mask(), dot(phi, phi_k_ref[strip.whole, :], 1, 1), 0.0)
        score_high[strip.at, :], score_low[strip.at, :] = split2(scores)

    gather_s.arrived()
    chain.sum_line(gathered, line)
    share_s.start()
    chain.from_line(gathered, moved)

    for strip in every:
        total_ref[strip.at, :] = dot(score_high[strip.at, :], values[strip.run], 1, 0) + dot(
            score_low[strip.at, :], values[strip.run], 1, 0
        )

    tell_s.arrived()
    totals = collector.collect(total_land)
    totals_high, totals_low = split2(totals)
    weights = []
    for strip in every:
        front, back = strip.sides()
        phi = phi_q_ref[strip.at, :]
        grad = strip.of(qg_ref)[:, HEAD_DIM:].astype(F32)
        far = dot(phi, totals_high, 1, 0) + dot(phi, totals_low, 1, 0)
        lane = 2 * strip.run
        denom = total_ref[strip.at, HEAD_DIM : HEAD_DIM + 1]
        denom = denom + jnp.where(front[:, :1], far[:, lane : lane + 1], 0.0)
        denom = denom + jnp.where(back[:, :1], far[:, lane + 1 : lane + 2], 0.0)
        inverse = 1.0 / denom
        inverse_ref[strip.at, :] = jnp.broadcast_to(inverse, (STRIP, LANES))
        a = grad * inverse
        a_ref[strip.at, :] = extended(a, jnp.zeros((STRIP, 1), F32))
        weights.append(split2(strip.pair(a, back, a, front)))
    store_pieces(piece_g, pieces_of(phi_q_ref, weights))
    gather_g.start()

    share_s.arrived()
    chain.from_lines(lines, moved)
    scatter_s.start()

    for run in range(2):
        whole = slice(run * run_rows, (run + 1) * run_rows)
        a_high, a_low = split2(a_ref[whole, :])
        both = dot(beside(a_high, a_low), score_high[whole, :], 0, 0)
        value_up_ref[:, whole] = both[:LANES] + both[LANES:] + dot(a_high, score_low[whole, :], 0, 0)

    gather_g.arrived()
    chain.sum_line(gathered_g, line_g)
    share_g.start()
    chain.from_line(gathered_g, moved_g)

    scatter_s.arrived()
    states = [split2(beside(sums, totals)) for sums in chain.sums(state)]
    weights = []
    for strip in every:
        front, back = strip.sides()
        phi = phi_q_ref[strip.at, :]
        grad = strip.of(qg_ref)[:, HEAD_DIM:].astype(F32)
        high, low = states[strip.run]
        far = dot(phi, high[:, :LANES], 1, 0) + dot(phi, low[:, :LANES], 1, 0)
        numer = total_ref[strip.at, :HEAD_DIM]
        numer = numer + jnp.where(front[:, :HEAD_DIM], far[:, :HEAD_DIM], 0.0)
        numer = numer + jnp.where(back[:, :HEAD_DIM], far[:, HEAD_DIM:], 0.0)
        inverse = inverse_ref[strip.at, :HEAD_DIM]
        attended = numer * inverse
        total_ref[strip.at, :HEAD_DIM] = attended
        bias = -jnp.sum(grad * attended, axis=1, keepdims=True) * inverse[:, :1]
        a_ref[strip.at, :] = extended(a_ref[strip.at, :HEAD_DIM], bias)
        weights.append(split2(strip.line(back, front, bias)))
    found = pieces_of(phi_q_ref, weights)
    total_send_g[...] = totals_in_rows(found[0] + found[1])
    tell_g.start()

    def query_part(strip):
        front, back = strip.sides()
        a = a_ref[strip.at, :]
        bias = a[:, HEAD_DIM : HEAD_DIM + 1]
        doubled = beside(values[strip.run], values[strip.run])
        coupling = jnp.where(strip.mask(), dot(beside(*split2(a)), doubled, 1, 1), 0.0)
        high, low = split2(coupling)
        coupling_high[strip.at, :] = high
        coupling_low[strip.at, :] = low
        phi_k = phi_k_ref[strip.whole, :]
        up = dot(high, phi_k, 1, 0) + dot(low, phi_k, 1, 0)
        vectors = a[:, :HEAD_DIM]
        use_high, use_low = split2(beside(strip.pair(vectors, front, vectors, back), strip.line(front, back, bias)))
        high, low = states[strip.run]
        up = up + dot(use_high, high, 1, 1) + dot(use_high, low, 1, 1) + dot(use_low, high, 1, 1)
        query_grad = feature_grad(strip.of(qg_ref)[:, :HEAD_DIM], expo_q_ref[strip.at, :], up, grad_parts)
        done = beside(total_ref[strip.at, :HEAD_DIM], query_grad).astype(BF16)
        done_q[strip.slots] = done.reshape(blocks, own, LANES)
    for strip in every[: strips // 2]:
        query_part(strip)

    share_g.arrived()
    chain.from_lines(lines_g, moved_g)
    scatter_g.start()

    for strip in every[strips // 2 :]:
        query_part(strip)
    give_q.start()

    for run in range(2):
        whole = slice(run * run_rows, (run + 1) * run_rows)
        phi = phi_q_ref[whole, :]
        key_up_ref[:, whole] = dot(phi, coupling_high[whole, :], 0, 0) + dot(phi, coupling_low[whole, :], 0, 0)

    scatter_g.arrived()
    tell_g.arrived()
    totals_g = collector.collect(total_land_g)
    states_g = [split2(beside(sums, totals_g)) for sums in chain.sums(state_g)]
    for strip in every:
        front, back = strip.sides()
        phi = phi_k_ref[strip.at, :]
        packed = strip.of(kv_ref)
        vectors = packed[:, HEAD_DIM:].astype(F32)
        use = beside(strip.pair(vectors, front, vectors, back), strip.line(front, back, ones)).astype(BF16)
        high, low = states_g[strip.run]
        up = jnp.transpose(key_up_ref[:, strip.at]) + dot(use, high, 1, 1) + dot(use, low, 1, 1)
        far = dot(phi, high[:, :LANES], 1, 0) + dot(phi, low[:, :LANES], 1, 0)
        total = jnp.transpose(value_up_ref[:, strip.at])[:, :HEAD_DIM]
        total = total + jnp.where(front[:, :HEAD_DIM], far[:, :HEAD_DIM], 0.0)
        total = total + jnp.where(back[:, :HEAD_DIM], far[:, HEAD_DIM:], 0.0)
        key_grad = feature_grad(packed[:, :HEAD_DIM], expo_k_ref[strip.at, :], up, grad_parts)
        done_k[strip.slots] = beside(key_grad, total).astype(BF16).reshape(blocks, own, LANES)
    give_k.start()

    give_q.arrived()
    first_ref[...] = back_q[...]
    give_k.arrived()
    second_ref[...] = back_k[...]
    for each in (
        move_kv, move_qg, gather_s, share_s, scatter_s, gather_g, share_g, scatter_g, give_q, give_k, tell_s, tell_g
    ):
        each.sent()


def body(coarse, fine, query_rows, key_rows, value_rows, out_grad, doc_lengths, projection):
    own = query_rows.shape[0]
    rows = own * fine
    shape = jax.ShapeDtypeStruct
    packed = shape((fine, own, LANES), BF16)
    share = FEATURES // LINE
    outer = coarse // LINE
    sources = 2 * LINE + outer
    vmem = pl.BlockSpec(memory_space=pltpu.VMEM)
    anywhere = pl.BlockSpec(memory_space=pl.ANY)
    tokens = pltpu.VMEM(query_rows.shape, BF16)
    blocks = pltpu.VMEM((fine, own, LANES), BF16)
    pieces = pltpu.VMEM((LINE, 2 * share, LANES), F32)
    results = pltpu.VMEM((LINE, 2 * share, LANES), F32)
    lines = [pltpu.VMEM((share, LANES), F32), pltpu.VMEM((outer, share, LANES), F32)]
    told = [pltpu.VMEM((4, LANES), F32), pltpu.VMEM((coarse, 4, LANES), F32)]
    phase = [pieces] * 2 + lines + [results] * 2
    coefs = [pltpu.VMEM(x + (LANES,), F32) for x in ((2 * LINE, sources), (sources,), (4, 2 * coarse))]
    narrow_rows = pltpu.VMEM((rows, LANES), BF16)
    wide_rows = pltpu.VMEM((rows, LANES), F32)
    square = pltpu.VMEM((rows, rows // 2), BF16)
    turned = pltpu.VMEM((LANES, rows), F32)
    scratch = [tokens] * 4 + [blocks] * 4 + phase * 2 + told * 2 + coefs + [blocks] * 4
    scratch += [narrow_rows] * 2 + [wide_rows] * 6 + [square] * 4 + [turned] * 2
    scratch += [pltpu.SemaphoreType.DMA((count,)) for count in (4, 12, 12)]
    scratch += [pltpu.SemaphoreType.REGULAR]
    first, second = pl.pallas_call(
        main_kernel,
        out_shape=(packed, packed),
        in_specs=[anywhere] * 4 + [vmem] * 2,
        out_specs=(vmem, vmem),
        scratch_shapes=scratch,
        compiler_params=pltpu.CompilerParams(
            collective_id=0, has_side_effects=True, vmem_limit_bytes=VMEM_BYTES
        ),
        cost_estimate=pl.CostEstimate(
            flops=2 * rows * rows * LANES * 6, bytes_accessed=8 * own * fine * HEAD_DIM * 2, transcendentals=0
        ),
    )(query_rows, key_rows, value_rows, out_grad, doc_lengths.reshape(-1, LANES), projection.T)
    out = shape(query_rows.shape, BF16)
    return pl.pallas_call(
        unpack_kernel,
        out_shape=(out, out, out, out),
        in_specs=[vmem] * 2,
        out_specs=(vmem,) * 4,
        compiler_params=pltpu.CompilerParams(vmem_limit_bytes=VMEM_BYTES),
        cost_estimate=pl.CostEstimate(flops=0, bytes_accessed=8 * own * fine * HEAD_DIM * 2, transcendentals=0),
    )(first, second)


def solution(mesh):
    tokens = P(("wide", "narrow"), None)
    return jax.shard_map(
        functools.partial(body, mesh.shape["wide"], mesh.shape["narrow"]),
        mesh=mesh,
        in_specs=(tokens, tokens, tokens, tokens, P(), P()),
        out_specs=(tokens, tokens, tokens, tokens),
        check_vma=False,
    )
```

```python
import functools

import jax
import jax.numpy as jnp
from jax import lax
from jax.experimental import pallas as pl
from jax.experimental.pallas import tpu as pltpu
from jax.sharding import PartitionSpec as P

HEAD_DIM = 64
FEATURES = 128
LANES = 128
FLOOR = 1e-06
F32 = jnp.float32
BF16 = jnp.bfloat16
INV_ROOT = HEAD_DIM ** (-0.25)
FACTOR = FEATURES ** (-0.5)
VMEM_BYTES = 56 * 1024 * 1024
MESH = pl.DeviceIdType.MESH
STRIP = 256
LINE = 8


def dot(a, b, da, db):
    return lax.dot_general(a, b, (((da,), (db,)), ((), ())), preferred_element_type=F32)


def split2(x):
    high = x.astype(BF16)
    return high, (x - high.astype(F32)).astype(BF16)


def split3(x):
    high = x.astype(BF16)
    rest = x - high.astype(F32)
    mid = rest.astype(BF16)
    return high, mid, (rest - mid.astype(F32)).astype(BF16)


def beside(*parts):
    return jnp.concatenate(parts, axis=1)


def features(x, parts):
    mixed = dot(beside(x, x, x, jnp.zeros_like(x)), parts, 1, 0)
    wide = x.astype(F32)
    half = jnp.sum(wide * wide, axis=1, keepdims=True) * (0.5 * INV_ROOT * INV_ROOT)
    expo = jnp.exp(mixed - half) * FACTOR
    return expo, (expo + FLOOR * FACTOR).astype(BF16)


def extended(x, extra):
    rows = x.shape[0]
    lane = lax.broadcasted_iota(jnp.int32, (rows, HEAD_DIM), 1)
    tail = jnp.where(lane == 0, jnp.broadcast_to(extra, (rows, HEAD_DIM)), 0.0)
    return jnp.concatenate([x, tail], axis=1)


def feature_grad(x, expo, up, parts):
    high, low = split2(expo * up)
    back = dot(beside(high, low), beside(parts[0], parts[0]), 1, 1) + dot(high, parts[1], 1, 1)
    scaled = x.astype(F32) * INV_ROOT
    return (back[:, :HEAD_DIM] - scaled * back[:, HEAD_DIM : HEAD_DIM + 1]) * INV_ROOT


def unpack_kernel(first_ref, second_ref, out_a, out_b, out_c, out_d):
    for pair in range(first_ref.shape[0] // 2):
        cols = slice(pair * LANES, (pair + 1) * LANES)
        for ref, left, right in ((first_ref, out_a, out_b), (second_ref, out_c, out_d)):
            even, odd = ref[2 * pair], ref[2 * pair + 1]
            left[:, cols] = jnp.concatenate([even[:, :HEAD_DIM], odd[:, :HEAD_DIM]], axis=1)
            right[:, cols] = jnp.concatenate([even[:, HEAD_DIM:], odd[:, HEAD_DIM:]], axis=1)


def ends_of(lengths):
    lines = lengths.shape[0]
    wide = lengths.astype(F32)
    high = wide.astype(BF16)
    low = (wide - high.astype(F32)).astype(BF16)
    row = lax.broadcasted_iota(jnp.int32, (LANES, LANES), 0)
    col = lax.broadcasted_iota(jnp.int32, (LANES, LANES), 1)
    upto = jnp.where(row <= col, 1.0, 0.0).astype(BF16)
    within = dot(high, upto, 1, 0) + dot(low, upto, 1, 0)
    offset = jnp.zeros((1, 1), F32)
    ends = []
    for line in range(lines):
        ends.append(within[line : line + 1] + offset)
        offset = ends[-1][:, LANES - 1 :]
    return ends


def count_ends(ends, positions):
    count = jnp.zeros((positions.shape[0], LANES), F32)
    for line in ends:
        count = count + jnp.where(line <= positions, 1.0, 0.0)
    return jnp.sum(count, axis=1, keepdims=True)


def lanes_of(rows):
    return lax.broadcasted_iota(jnp.int32, (rows, LANES), 1)


def totals_in_rows(totals):
    return jnp.transpose(totals)[:4]


def run_of(slot, groups):
    second = jnp.where(slot >= groups, 1, 0)
    group = slot - second * groups
    odd = lax.rem(group, 2)
    return (group - odd) * 2 + odd + second * 2


def relation(own, others):
    start_r, first_r, last_r = own
    start, first, last = others
    rising = (last == first_r) & (start < start_r)
    falling = (first == last_r) & (start > start_r)
    return jnp.where(rising, 1.0, 0.0), jnp.where(falling, 1.0, 0.0)


def spans(ends, index, run_rows, length):
    start = (index * run_rows).astype(F32)
    found = (start, count_ends(ends, start), count_ends(ends, start + length - 1.0))
    return tuple(jnp.broadcast_to(x, (index.shape[0], LANES)) for x in found)


class Totals:
    def __init__(self, ends, here, run_rows, groups, coef, ids_of):
        self.groups, self.coef = groups, coef
        slot = lax.broadcasted_iota(jnp.int32, (2 * groups, 1), 0)
        others = spans(ends, run_of(slot, groups), run_rows, float(run_rows))
        for run in range(2):
            begin = ((here.first_run + 2 * run) * run_rows).astype(F32)
            coef[2 * run], coef[2 * run + 1] = relation((begin, *ids_of(run)), others)

    def collect(self, landed):
        rows = []
        sides = [jnp.concatenate([landed[:, side, :], landed[:, 2 + side, :]], axis=0) for side in range(2)]
        for row in range(4):
            rows.append(jnp.sum(self.coef[row] * sides[row % 2], axis=0, keepdims=True))
        return jnp.transpose(jnp.concatenate(rows + [jnp.zeros((LANES - 4, LANES), F32)], axis=0))


class Chain:
    def __init__(self, ends, here, run_rows, inner, outer, row_coef, line_coef):
        self.inner, self.outer, self.share = inner, outer, FEATURES // inner
        self.row_coef, self.line_coef = row_coef, line_coef
        runs = 2 * inner
        size = runs + outer
        slot = lax.broadcasted_iota(jnp.int32, (size, 1), 0)
        odd = jnp.where(lax.rem(slot, 4) >= 2, 1, 0)
        of_run = here.line * runs + slot + lax.rem(slot, 2) - odd
        index = jnp.where(slot < runs, of_run, (slot - runs) * runs)
        length = jnp.where(slot < runs, run_rows, run_rows * runs).astype(F32)
        others = spans(ends, index, run_rows, length)
        start, first, last = others
        valid = jnp.broadcast_to(slot - runs, (size, LANES)) != here.line
        left = lanes_of(size) < HEAD_DIM
        for run in range(runs):
            rising, falling = relation([x[run : run + 1] for x in others], others)
            row_coef[run] = jnp.where(valid, jnp.where(left, rising, falling), 0.0)
        ending = jnp.where(last == last[runs - 1 : runs], 1.0, 0.0)
        line_coef[...] = jnp.where(left, ending, jnp.where(first == first[:1], 1.0, 0.0))

    def block(self, gathered, run):
        return gathered[run // 2, (run % 2) * self.share : (run % 2 + 1) * self.share, :]

    def sum_line(self, gathered, out):
        found = jnp.zeros((self.share, LANES), F32)
        for run in range(2 * self.inner):
            found = found + self.line_coef[run : run + 1, :] * self.block(gathered, run)
        out[...] = found

    def place(self, run):
        return run // 2, slice((run % 2) * self.share, (run % 2 + 1) * self.share)

    def from_line(self, gathered, out):
        runs = 2 * self.inner
        blocks = [self.block(gathered, run) for run in range(runs)]
        for run in range(runs):
            found = jnp.zeros((self.share, LANES), F32)
            for source in range(runs):
                if source != run:
                    found = found + self.row_coef[run, source : source + 1, :] * blocks[source]
            owner, at = self.place(run)
            out[owner, at, :] = found

    def from_lines(self, lines, out):
        runs = 2 * self.inner
        blocks = [lines[line] for line in range(self.outer)]
        for run in range(runs):
            owner, at = self.place(run)
            found = out[owner, at, :]
            for line in range(self.outer):
                source = runs + line
                found = found + self.row_coef[run, source : source + 1, :] * blocks[line]
            out[owner, at, :] = found

    def sums(self, state):
        return [
            state[:, run * self.share : (run + 1) * self.share, :].reshape(FEATURES, LANES) for run in range(2)
        ]


def store_pieces(ref, sums):
    owners = ref.shape[0]
    share = FEATURES // owners
    for run in range(2):
        ref[:, run * share : (run + 1) * share, :] = sums[run].reshape(owners, share, LANES)


def over_peers(size, step):
    group = 7 if (size - 1) % 7 == 0 else 1

    def several(turn, carry):
        for i in range(group):
            step(turn * group + i + 1)
        return carry

    lax.fori_loop(0, (size - 1) // group, several, 0)


class Place:
    def __init__(self):
        self.wide = lax.axis_index("wide")
        self.narrow = lax.axis_index("narrow")
        self.second = lax.rem(self.wide, 2)
        self.quarter = lax.rem(self.narrow, 4)
        self.half = lax.div(self.narrow, 4)
        self.even = self.wide - self.second
        self.member = self.second * 4 + self.quarter
        self.line = lax.div(self.wide, LINE)
        self.base = self.line * LINE
        self.inside = self.even - self.base + self.half
        self.group = self.even + self.half
        self.first_run = 2 * self.even + self.half

    def of_member(self, member):
        quarter = lax.rem(member, 4)
        return {"wide": self.even + lax.div(member, 4), "narrow": self.half * 4 + quarter}

    def of_inside(self, inside):
        half = lax.rem(inside, 2)
        return {"wide": self.base + inside - half + self.second, "narrow": half * 4 + self.quarter}

    def of_group(self, group):
        half = lax.rem(group, 2)
        return {"wide": group - half + self.second, "narrow": half * 4 + self.quarter}

    def of_line(self, line):
        return {"wide": self.wide - self.base + line * LINE, "narrow": self.narrow}


class Exchange:
    def __init__(self, me, device_of, send, land, send_sem, recv_sem, same=False):
        self.me, self.device_of, self.size, self.same = me, device_of, land.shape[0], same
        self.send, self.land, self.send_sem, self.recv_sem = send, land, send_sem, recv_sem

    def start(self):
        def step(offset):
            peer = lax.rem(self.me + offset, self.size)
            pltpu.make_async_remote_copy(
                src_ref=self.send if self.same else self.send.at[peer],
                dst_ref=self.land.at[self.me],
                send_sem=self.send_sem,
                recv_sem=self.recv_sem,
                device_id=self.device_of(peer),
                device_id_type=MESH,
            ).start()

        over_peers(self.size, step)
        self.land[self.me] = self.send[...] if self.same else self.send[self.me]

    def all_but_one(self):
        part = self.land.at[pl.ds(0, self.size - 1)]
        return pltpu.make_async_remote_copy(
            src_ref=part,
            dst_ref=part,
            send_sem=self.send_sem,
            recv_sem=self.recv_sem,
            device_id=self.device_of(lax.rem(self.me + 1, self.size)),
            device_id_type=MESH,
        )

    def arrived(self):
        self.all_but_one().wait_recv()

    def sent(self):
        self.all_but_one().wait_send()


def main_kernel(
    q_any, k_any, v_any, g_any, lengths_ref, proj_ref,
    first_ref, second_ref,
    q_ref, k_ref, v_ref, g_ref,
    kv_send, kv_ref, qg_send, qg_ref,
    piece, gathered, line, lines, moved, state, piece_g, gathered_g, line_g, lines_g, moved_g, state_g,
    total_send, total_land, total_send_g, total_land_g,
    row_coef, line_coef, own_coef,
    done_q, back_q, done_k, back_k,
    phi_k_ref, phi_q_ref, expo_k_ref, expo_q_ref, ids_ref, a_ref, total_ref, inverse_ref,
    score_high, score_low, coupling_high, coupling_low, key_up_ref, value_up_ref,
    in_sem, send_sem, recv_sem, line_sem,
):
    fine = kv_send.shape[0]
    inner, outer, coarse = piece.shape[0], lines.shape[0], total_land.shape[0]
    own = q_ref.shape[0]
    rows = own * fine
    run_rows = rows // 2
    strips = rows // STRIP
    blocks = STRIP // own
    here = Place()

    def within(number, send, land):
        return Exchange(here.member, here.of_member, send, land, send_sem.at[number], recv_sem.at[number])

    def across(number, send, land):
        return Exchange(here.inside, here.of_inside, send, land, send_sem.at[number], recv_sem.at[number])

    def lengthwise(number, send, land):
        return Exchange(here.line, here.of_line, send, land, send_sem.at[number], recv_sem.at[number], True)

    def everywhere(number, send, land):
        return Exchange(here.group, here.of_group, send, land, send_sem.at[number], recv_sem.at[number], True)

    move_kv = within(0, kv_send, kv_ref)
    move_qg = within(1, qg_send, qg_ref)
    gather_s = across(2, piece, gathered)
    share_s = lengthwise(3, line, lines)
    scatter_s = across(4, moved, state)
    gather_g = across(5, piece_g, gathered_g)
    share_g = lengthwise(6, line_g, lines_g)
    scatter_g = across(7, moved_g, state_g)
    give_q = within(8, done_q, back_q)
    give_k = within(9, done_k, back_k)
    tell_s = everywhere(10, total_send, total_land)
    tell_g = everywhere(11, total_send_g, total_land_g)

    barrier = pltpu.get_barrier_semaphore()

    def greet(sem, me, device_of, size):
        def step(offset):
            pl.semaphore_signal(
                sem, inc=1, device_id=device_of(lax.rem(me + offset, size)), device_id_type=MESH
            )

        over_peers(size, step)

    loads = [
        pltpu.make_async_copy(source, target, in_sem.at[i])
        for i, (source, target) in enumerate(
            ((k_any, k_ref), (v_any, v_ref), (q_any, q_ref), (g_any, g_ref))
        )
    ]
    for load in loads:
        load.start()
    greet(barrier, here.member, here.of_member, fine)
    greet(barrier, here.inside, here.of_inside, inner)
    greet(barrier, here.line, here.of_line, outer)

    def pack(left, right, target):
        for head in range(fine):
            cols = slice(head * HEAD_DIM, (head + 1) * HEAD_DIM)
            target[head] = beside(left[:, cols], right[:, cols])

    loads[0].wait()
    loads[1].wait()
    pack(k_ref, v_ref, kv_send)
    pl.semaphore_wait(barrier, fine + inner + outer - 3)
    move_kv.start()
    greet(line_sem, here.line, here.of_line, outer)
    loads[2].wait()
    loads[3].wait()
    pack(q_ref, g_ref, qg_send)
    move_qg.start()

    projection = proj_ref[...]
    parts = split3(projection * INV_ROOT)
    mix_parts = jnp.concatenate([parts[0], parts[1], parts[2], jnp.zeros_like(parts[0])], axis=0)
    below = lax.broadcasted_iota(jnp.int32, projection.shape, 0) == 0
    grad_parts = split2(jnp.concatenate([projection, jnp.where(below, 1.0, 0.0)], axis=0))

    ends = ends_of(lengths_ref[...])

    class Strip:
        def __init__(self, number):
            self.at = slice(number * STRIP, (number + 1) * STRIP)
            self.slots = slice(number * blocks, (number + 1) * blocks)
            self.run = number * STRIP // run_rows
            self.whole = slice(self.run * run_rows, (self.run + 1) * run_rows)
            inside = number * STRIP - self.run * run_rows
            start = ((here.first_run + 2 * self.run) * run_rows + inside).astype(F32)
            self.places = lax.broadcasted_iota(jnp.int32, (STRIP, 1), 0).astype(F32) + start

        def of(self, ref):
            return ref[self.slots].reshape(STRIP, LANES)

        def sides(self):
            ids = ids_ref[self.at, :]
            ends_at = self.whole
            return ids == ids_ref[ends_at.start : ends_at.start + 1, :], ids == ids_ref[ends_at.stop - 1 : ends_at.stop, :]

        def mask(self):
            return ids_ref[self.at, :1] == id_row[:, self.whole]

        def pair(self, left, left_use, right, right_use):
            return beside(
                jnp.where(left_use[:, :HEAD_DIM], left, 0.0), jnp.where(right_use[:, :HEAD_DIM], right, 0.0)
            )

        def line(self, left_use, right_use, amount):
            lane = lanes_of(STRIP) - 2 * self.run
            use = ((lane == 0) & left_use) | ((lane == 1) & right_use)
            return jnp.where(use, jnp.broadcast_to(amount, (STRIP, LANES)), 0.0)

    every = [Strip(number) for number in range(strips)]
    for strip in every:
        ids_ref[strip.at, :] = jnp.broadcast_to(count_ends(ends, strip.places), (STRIP, LANES))
    id_row = jnp.transpose(ids_ref[...])[:1, :]
    ones = jnp.ones((STRIP, 1), F32)

    def ids_of(run):
        begin, end = run * run_rows, (run + 1) * run_rows
        return ids_ref[begin : begin + 1, :], ids_ref[end - 1 : end, :]

    chain = Chain(ends, here, run_rows, inner, outer, row_coef, line_coef)
    collector = Totals(ends, here, run_rows, coarse, own_coef, ids_of)

    def pieces_of(phi_ref, weights):
        result = []
        for run in range(2):
            found = 0.0
            for strip, weight in zip(every, weights):
                if strip.run == run:
                    for part in weight:
                        found = found + dot(phi_ref[strip.at, :], part, 0, 0)
            result.append(found)
        return result

    move_kv.arrived()
    weights = []
    for strip in every:
        packed = strip.of(kv_ref)
        expo, phi = features(packed[:, :HEAD_DIM], mix_parts)
        expo_k_ref[strip.at, :] = expo
        phi_k_ref[strip.at, :] = phi
        front, back = strip.sides()
        vectors = packed[:, HEAD_DIM:].astype(F32)
        weights.append([beside(strip.pair(vectors, back, vectors, front), strip.line(back, front, ones)).astype(BF16)])
    found = pieces_of(phi_k_ref, weights)
    store_pieces(piece, [x[:, :LANES] for x in found])
    gather_s.start()
    total_send[...] = totals_in_rows(found[0][:, LANES:] + found[1][:, LANES:])
    pl.semaphore_wait(line_sem, outer - 1)
    tell_s.start()

    def values_of(run):
        packed = kv_ref[run * fine // 2 : (run + 1) * fine // 2].reshape(run_rows, LANES)
        return extended(packed[:, HEAD_DIM:].astype(F32), jnp.ones((run_rows, 1), F32)).astype(BF16)

    values = [values_of(run) for run in range(2)]

    move_qg.arrived()
    for strip in every:
        expo, phi = features(strip.of(qg_ref)[:, :HEAD_DIM], mix_parts)
        expo_q_ref[strip.at, :] = expo
        phi_q_ref[strip.at, :] = phi
        scores = jnp.where(strip.mask(), dot(phi, phi_k_ref[strip.whole, :], 1, 1), 0.0)
        score_high[strip.at, :], score_low[strip.at, :] = split2(scores)

    gather_s.arrived()
    chain.sum_line(gathered, line)
    share_s.start()
    chain.from_line(gathered, moved)

    for strip in every:
        total_ref[strip.at, :] = dot(score_high[strip.at, :], values[strip.run], 1, 0) + dot(
            score_low[strip.at, :], values[strip.run], 1, 0
        )

    tell_s.arrived()
    totals = collector.collect(total_land)
    totals_high, totals_low = split2(totals)
    weights = []
    for strip in every:
        front, back = strip.sides()
        phi = phi_q_ref[strip.at, :]
        grad = strip.of(qg_ref)[:, HEAD_DIM:].astype(F32)
        far = dot(phi, totals_high, 1, 0) + dot(phi, totals_low, 1, 0)
        lane = 2 * strip.run
        denom = total_ref[strip.at, HEAD_DIM : HEAD_DIM + 1]
        denom = denom + jnp.where(front[:, :1], far[:, lane : lane + 1], 0.0)
        denom = denom + jnp.where(back[:, :1], far[:, lane + 1 : lane + 2], 0.0)
        inverse = 1.0 / denom
        inverse_ref[strip.at, :] = jnp.broadcast_to(inverse, (STRIP, LANES))
        a = grad * inverse
        a_ref[strip.at, :] = extended(a, jnp.zeros((STRIP, 1), F32))
        weights.append(split2(strip.pair(a, back, a, front)))
    store_pieces(piece_g, pieces_of(phi_q_ref, weights))
    gather_g.start()

    share_s.arrived()
    chain.from_lines(lines, moved)
    scatter_s.start()

    for run in range(2):
        whole = slice(run * run_rows, (run + 1) * run_rows)
        a_high, a_low = split2(a_ref[whole, :])
        both = dot(beside(a_high, a_low), score_high[whole, :], 0, 0)
        value_up_ref[whole, :] = jnp.transpose(
            both[:LANES] + both[LANES:] + dot(a_high, score_low[whole, :], 0, 0)
        )

    gather_g.arrived()
    chain.sum_line(gathered_g, line_g)
    share_g.start()
    chain.from_line(gathered_g, moved_g)

    scatter_s.arrived()
    states = [split2(beside(sums, totals)) for sums in chain.sums(state)]
    weights = []
    for strip in every:
        front, back = strip.sides()
        phi = phi_q_ref[strip.at, :]
        grad = strip.of(qg_ref)[:, HEAD_DIM:].astype(F32)
        high, low = states[strip.run]
        far = dot(phi, high[:, :LANES], 1, 0) + dot(phi, low[:, :LANES], 1, 0)
        numer = total_ref[strip.at, :HEAD_DIM]
        numer = numer + jnp.where(front[:, :HEAD_DIM], far[:, :HEAD_DIM], 0.0)
        numer = numer + jnp.where(back[:, :HEAD_DIM], far[:, HEAD_DIM:], 0.0)
        inverse = inverse_ref[strip.at, :HEAD_DIM]
        attended = numer * inverse
        total_ref[strip.at, :HEAD_DIM] = attended
        bias = -jnp.sum(grad * attended, axis=1, keepdims=True) * inverse[:, :1]
        a_ref[strip.at, :] = extended(a_ref[strip.at, :HEAD_DIM], bias)
        weights.append(split2(strip.line(back, front, bias)))
    found = pieces_of(phi_q_ref, weights)
    total_send_g[...] = totals_in_rows(found[0] + found[1])
    tell_g.start()

    def query_part(strip):
        front, back = strip.sides()
        a = a_ref[strip.at, :]
        bias = a[:, HEAD_DIM : HEAD_DIM + 1]
        doubled = beside(values[strip.run], values[strip.run])
        coupling = jnp.where(strip.mask(), dot(beside(*split2(a)), doubled, 1, 1), 0.0)
        high, low = split2(coupling)
        coupling_high[strip.at, :] = high
        coupling_low[strip.at, :] = low
        phi_k = phi_k_ref[strip.whole, :]
        up = dot(high, phi_k, 1, 0) + dot(low, phi_k, 1, 0)
        vectors = a[:, :HEAD_DIM]
        use_high, use_low = split2(beside(strip.pair(vectors, front, vectors, back), strip.line(front, back, bias)))
        high, low = states[strip.run]
        up = up + dot(use_high, high, 1, 1) + dot(use_high, low, 1, 1) + dot(use_low, high, 1, 1)
        query_grad = feature_grad(strip.of(qg_ref)[:, :HEAD_DIM], expo_q_ref[strip.at, :], up, grad_parts)
        done = beside(total_ref[strip.at, :HEAD_DIM], query_grad).astype(BF16)
        done_q[strip.slots] = done.reshape(blocks, own, LANES)
    for strip in every[: strips // 2]:
        query_part(strip)

    share_g.arrived()
    chain.from_lines(lines_g, moved_g)
    scatter_g.start()

    for strip in every[strips // 2 :]:
        query_part(strip)
    give_q.start()

    for run in range(2):
        whole = slice(run * run_rows, (run + 1) * run_rows)
        phi = phi_q_ref[whole, :]
        key_up_ref[whole, :] = jnp.transpose(
            dot(phi, coupling_high[whole, :], 0, 0) + dot(phi, coupling_low[whole, :], 0, 0)
        )

    scatter_g.arrived()
    sums_g = chain.sums(state_g)
    for strip in every:
        front, back = strip.sides()
        phi = phi_k_ref[strip.at, :]
        high, low = split2(sums_g[strip.run])
        far = dot(phi, high, 1, 0) + dot(phi, low, 1, 0)
        total = value_up_ref[strip.at, :HEAD_DIM]
        total = total + jnp.where(front[:, :HEAD_DIM], far[:, :HEAD_DIM], 0.0)
        value_up_ref[strip.at, :HEAD_DIM] = total + jnp.where(back[:, :HEAD_DIM], far[:, HEAD_DIM:], 0.0)

    tell_g.arrived()
    totals_g = collector.collect(total_land_g)
    states_g = [split2(beside(sums, totals_g)) for sums in sums_g]
    for strip in every:
        front, back = strip.sides()
        packed = strip.of(kv_ref)
        vectors = packed[:, HEAD_DIM:].astype(F32)
        use = beside(strip.pair(vectors, front, vectors, back), strip.line(front, back, ones)).astype(BF16)
        high, low = states_g[strip.run]
        up = key_up_ref[strip.at, :] + dot(use, high, 1, 1) + dot(use, low, 1, 1)
        key_grad = feature_grad(packed[:, :HEAD_DIM], expo_k_ref[strip.at, :], up, grad_parts)
        done = beside(key_grad, value_up_ref[strip.at, :HEAD_DIM]).astype(BF16)
        done_k[strip.slots] = done.reshape(blocks, own, LANES)
    give_k.start()

    give_q.arrived()
    first_ref[...] = back_q[...]
    give_k.arrived()
    second_ref[...] = back_k[...]
    for each in (
        move_kv, move_qg, gather_s, share_s, scatter_s, gather_g, share_g, scatter_g, give_q, give_k, tell_s, tell_g
    ):
        each.sent()


def body(coarse, fine, query_rows, key_rows, value_rows, out_grad, doc_lengths, projection):
    own = query_rows.shape[0]
    rows = own * fine
    shape = jax.ShapeDtypeStruct
    packed = shape((fine, own, LANES), BF16)
    share = FEATURES // LINE
    outer = coarse // LINE
    sources = 2 * LINE + outer
    vmem = pl.BlockSpec(memory_space=pltpu.VMEM)
    anywhere = pl.BlockSpec(memory_space=pl.ANY)
    tokens = pltpu.VMEM(query_rows.shape, BF16)
    blocks = pltpu.VMEM((fine, own, LANES), BF16)
    pieces = pltpu.VMEM((LINE, 2 * share, LANES), F32)
    results = pltpu.VMEM((LINE, 2 * share, LANES), F32)
    lines = [pltpu.VMEM((share, LANES), F32), pltpu.VMEM((outer, share, LANES), F32)]
    told = [pltpu.VMEM((4, LANES), F32), pltpu.VMEM((coarse, 4, LANES), F32)]
    phase = [pieces] * 2 + lines + [results] * 2
    coefs = [pltpu.VMEM(x + (LANES,), F32) for x in ((2 * LINE, sources), (sources,), (4, 2 * coarse))]
    narrow_rows = pltpu.VMEM((rows, LANES), BF16)
    wide_rows = pltpu.VMEM((rows, LANES), F32)
    square = pltpu.VMEM((rows, rows // 2), BF16)
    scratch = [tokens] * 4 + [blocks] * 4 + phase * 2 + told * 2 + coefs + [blocks] * 4
    scratch += [narrow_rows] * 2 + [wide_rows] * 6 + [square] * 4 + [wide_rows] * 2
    scratch += [pltpu.SemaphoreType.DMA((count,)) for count in (4, 12, 12)]
    scratch += [pltpu.SemaphoreType.REGULAR]
    first, second = pl.pallas_call(
        main_kernel,
        out_shape=(packed, packed),
        in_specs=[anywhere] * 4 + [vmem] * 2,
        out_specs=(vmem, vmem),
        scratch_shapes=scratch,
        compiler_params=pltpu.CompilerParams(
            collective_id=0, has_side_effects=True, vmem_limit_bytes=VMEM_BYTES
        ),
        cost_estimate=pl.CostEstimate(
            flops=2 * rows * rows * LANES * 6, bytes_accessed=8 * own * fine * HEAD_DIM * 2, transcendentals=0
        ),
    )(query_rows, key_rows, value_rows, out_grad, doc_lengths.reshape(-1, LANES), projection.T)
    out = shape(query_rows.shape, BF16)
    return pl.pallas_call(
        unpack_kernel,
        out_shape=(out, out, out, out),
        in_specs=[vmem] * 2,
        out_specs=(vmem,) * 4,
        compiler_params=pltpu.CompilerParams(vmem_limit_bytes=VMEM_BYTES),
        cost_estimate=pl.CostEstimate(flops=0, bytes_accessed=8 * own * fine * HEAD_DIM * 2, transcendentals=0),
    )(first, second)


def solution(mesh):
    tokens = P(("wide", "narrow"), None)
    return jax.shard_map(
        functools.partial(body, mesh.shape["wide"], mesh.shape["narrow"]),
        mesh=mesh,
        in_specs=(tokens, tokens, tokens, tokens, P(), P()),
        out_specs=(tokens, tokens, tokens, tokens),
        check_vma=False,
    )
```
